32 devices in a mesh: groups: 2 (over y), dp: 4 (over z), fsdp: 4 (over x, core).
Axes of the slice: x: 2, y: 2, z: 4, core: 2. Of those that a mesh axis runs over, the one named last changes fastest.
Arguments:
- activations: bfloat16 [6144, 28672], P(('groups', 'dp'), 'fsdp'), parts along dimension 0, may hold values from -6 to 6
- out_grad: bfloat16 [6144, 8192], P(('groups', 'dp'), 'fsdp'), parts along dimension 0, may hold values from -0.0059814453 to 0.0059814453
- basis: bfloat16 [16384, 128], P('groups'), parts along dimension 0, may hold values from -0.5 to 0.5
- first_moment: float32 [57344, 128], P(('groups', 'fsdp', 'dp')), parts along dimension 0, may hold values from -0.6 to 0.6
- second_moment: float32 [57344, 128], P(('groups', 'fsdp', 'dp')), parts along dimension 0, may hold values from 0.0001 to 0.001
Outputs:
- update: bfloat16 [57344, 8192], P(('groups', 'fsdp'), 'dp'), parts along dimension 0
- first_next: float32 [57344, 128], P(('groups', 'fsdp', 'dp')), parts along dimension 0
- second_next: float32 [57344, 128], P(('groups', 'fsdp', 'dp')), parts along dimension 0
The draws below stay inside these ranges and needn't reach their ends.
There are 2 independent parts, one for each index of `groups`. The reference program is written for one: setup_inputs(seed, part) draws one part's arguments, and reference() takes and returns one part's arrays. A program takes and returns all parts, laid end to end along the dimension named above; each array names one. Nothing has to cross between parts.
All inputs are finite; a program needn't handle non-finite values.
Results may differ from the reference program's by a relative error of at most 0.0049.
The reference program's roundings to bfloat16 on the way (of `projected` and `normed`) count: a program that leaves them out, or rounds other values in their place, can miss the bound.
Values may be sent and summed in bfloat16 or wider, within the bound.
No kernel may reach another device: no remote copies, remote signals or barrier semaphores. Data moves between devices by JAX's collectives and lax.ppermute only.
A program may use at most 128 MiB of HBM per device.

```python
import math
import jax
import jax.numpy as jnp
from jax import lax

D = 8192
FF = 28672
R = 128
STEP = 10
TOKENS = 3072


def spiked(entries, rng, source, target, shards_of, factor):
    owner, partner = [(jnp.arange(entries.shape[position]) // (entries.shape[position] // shards_of)).reshape([-1 if axis == position else 1 for axis in range(entries.ndim)]) for position in (source, target)]
    chosen = jax.random.permutation(rng, shards_of)[partner]
    strong = (owner == chosen) | (owner == (partner + shards_of // 2) % shards_of)
    return jnp.where(strong, factor * entries, entries)


def steps_of(own_key, shape, shards, least, high):
    gain, own = 1.0, jax.random.fold_in(own_key, 6)
    for axis_at, blocks in shards:
        draws = jnp.exp(jax.random.uniform(jax.random.fold_in(own, axis_at), (blocks,), jnp.float32, least / len(shards), high / len(shards)))
        gain = gain * jnp.repeat(draws, shape[axis_at] // blocks).reshape([-1 if axis == axis_at else 1 for axis in range(len(shape))])
    return gain


def noise(key, shape, deviation, reach, split=(), kind=jnp.bfloat16):
    entries = deviation * jax.random.normal(key, shape, jnp.float32)
    if split:
        entries = entries * steps_of(key, shape, split, -0.22, 0.18)
    return jnp.clip(entries, -reach, reach).astype(kind)


def gaussian_with(stream_key, extent, scale, limit, cuts, heavy, kind=jnp.bfloat16):
    drawn = scale * jax.random.normal(stream_key, extent, jnp.float32)
    if cuts:
        drawn = drawn * steps_of(stream_key, extent, cuts, -0.22, 0.18)
    return jnp.clip(spiked(drawn, jax.random.fold_in(stream_key, 3), *heavy), -limit, limit).astype(kind)


def setup_inputs(seed: int = 0, part: int = 0) -> dict:
    seeds = jax.random.split(jax.random.key(seed), 6)
    part_keys = jax.random.split(jax.random.fold_in(seeds[5], part), 6)
    return {
        "activations": gaussian_with(part_keys[0], (TOKENS, FF), 1.0, 6.0, ((0, 4), (1, 4)), (0, 1, 4, 2.0)),
        "out_grad": noise(part_keys[1], (TOKENS, D), 0.001, 0.0059814453, ((0, 4), (1, 4))),
        "basis": noise(part_keys[2], (D, R), R ** -0.5, 0.5),
        "first_moment": noise(part_keys[3], (FF, R), 0.1, 0.6, ((0, 16),), jnp.float32),
        "second_moment": jnp.clip(jnp.exp(math.log(0.001) - 2.3025852 * jax.random.uniform(part_keys[4], (FF, R), jnp.float32) ** steps_of(part_keys[4], (FF, R), ((0, 16),), -0.2, 0.2)), 0.0001, 0.001),
    }


def reference(activations, out_grad, basis, first_moment, second_moment):
    projected = jnp.dot(out_grad, basis, preferred_element_type=jnp.float32).astype(jnp.bfloat16)
    low_grad = lax.dot_general(activations, projected, (((0,), (0,)), ((), ())), preferred_element_type=jnp.float32)
    first_next = 0.9 * first_moment + 0.1 * low_grad
    second_next = 0.999 * second_moment + 0.001 * low_grad * low_grad
    first_fix = 1.0 - 0.9 ** STEP
    second_fix = 1.0 - 0.999 ** STEP
    normed = (first_next / first_fix / (jnp.sqrt(second_next / second_fix) + 1e-08)).astype(jnp.bfloat16)
    update = lax.dot_general(normed, basis, (((1,), (1,)), ((), ())), preferred_element_type=jnp.float32)
    update = (0.25 * update).astype(jnp.bfloat16)
    return (update, first_next, second_next)
```

```python
import functools

import jax
import jax.numpy as jnp
from jax import lax
from jax.experimental import pallas as pl
from jax.experimental.pallas import tpu as pltpu
from jax.sharding import PartitionSpec as P

STEP = 10
CHUNKS = 2
VMEM = 16 << 20
WIDE = 32 << 20
PIECES = 3
TOKEN = jax.ShapeDtypeStruct((8, 128), jnp.float32)


def cost(flops, moved):
    return pl.CostEstimate(flops=flops, bytes_accessed=moved, transcendentals=0)


def swap(value, axis, bit):
    n = lax.axis_size(axis)
    return lax.ppermute(value, axis, [(i, i ^ bit) for i in range(n)])


def project(out_grad, basis):
    tokens, features = out_grad.shape
    rows, rank = tokens // 2, basis.shape[1]

    def kernel(grad_hbm, basis_hbm, give_ref, keep_ref, grad, base, sems):
        place = lax.axis_index("fsdp")
        core = lax.rem(place, 2)
        copies = [
            pltpu.make_async_copy(
                basis_hbm.at[pl.ds(pl.multiple_of(place * features, features), features), :],
                base,
                sems.at[0],
            )
        ]
        piece = rows // PIECES
        for turn, half in enumerate((1 - core, core)):
            for part in range(PIECES):
                first = half * rows + part * piece
                copies.append(
                    pltpu.make_async_copy(
                        grad_hbm.at[pl.ds(pl.multiple_of(first, piece), piece), :],
                        grad.at[turn, pl.ds(part * piece, piece), :],
                        sems.at[turn * PIECES + part + 1],
                    )
                )
        for copy in copies:
            copy.start()
        copies[0].wait()
        for turn, out_ref in enumerate((give_ref, keep_ref)):
            for part in range(PIECES):
                copies[turn * PIECES + part + 1].wait()
            out_ref[...] = jnp.dot(
                grad[turn], base[...], preferred_element_type=jnp.float32
            ).T

    return pl.pallas_call(
        kernel,
        in_specs=[pl.BlockSpec(memory_space=pltpu.HBM)] * 2,
        out_specs=[pl.BlockSpec(memory_space=pltpu.VMEM)] * 2,
        out_shape=[jax.ShapeDtypeStruct((rank, rows), jnp.float32)] * 2,
        scratch_shapes=[
            pltpu.VMEM((2, rows, features), jnp.bfloat16),
            pltpu.VMEM((features, rank), jnp.bfloat16),
            pltpu.SemaphoreType.DMA((2 * PIECES + 1,)),
        ],
        compiler_params=pltpu.CompilerParams(vmem_limit_bytes=WIDE),
        cost_estimate=cost(2 * tokens * features * rank, 2 * features * (tokens + rank)),
        name="project",
    )(out_grad, basis)


def settle(pair, far, after):
    def kernel(pair_ref, far_ref, after_ref, out_ref):
        out_ref[...] = (pair_ref[...] + far_ref[...]).astype(jnp.bfloat16)

    return pl.pallas_call(
        kernel,
        in_specs=[pl.BlockSpec(memory_space=pltpu.VMEM)] * 2
        + [pl.BlockSpec(memory_space=pl.ANY)],
        out_specs=pl.BlockSpec(memory_space=pltpu.VMEM),
        out_shape=jax.ShapeDtypeStruct(pair.shape, jnp.bfloat16),
        compiler_params=pltpu.CompilerParams(vmem_limit_bytes=VMEM),
        cost_estimate=cost(pair.size, 10 * pair.size),
        name="settle",
    )(pair, far, after)


def blocks_of(act_hbm, held, sems, parts, rows):
    copies = []
    for place, (bit, chunk) in enumerate(parts):
        block = (lax.axis_index("dp") ^ bit) * CHUNKS + chunk
        copies.append(
            pltpu.make_async_copy(
                act_hbm.at[:, pl.ds(pl.multiple_of(block * rows, 128), rows)],
                held.at[place],
                sems.at[place],
            )
        )
    for copy in copies:
        copy.start()
    return copies


def load(activations, parts, after):
    tokens, units = activations.shape
    rows = units // (lax.axis_size("dp") * CHUNKS)

    def kernel(act_hbm, after_ref, held, token_ref, sems):
        for copy in blocks_of(act_hbm, held, sems, parts, rows):
            copy.wait()
        token_ref[...] = jnp.zeros_like(token_ref)

    return pl.pallas_call(
        kernel,
        in_specs=[pl.BlockSpec(memory_space=pltpu.HBM), pl.BlockSpec(memory_space=pl.ANY)],
        out_specs=[pl.BlockSpec(memory_space=pltpu.VMEM)] * 2,
        out_shape=[jax.ShapeDtypeStruct((len(parts), tokens, rows), jnp.bfloat16), TOKEN],
        scratch_shapes=[pltpu.SemaphoreType.DMA((len(parts),))],
        compiler_params=pltpu.CompilerParams(vmem_limit_bytes=VMEM),
        cost_estimate=cost(0, 2 * tokens * rows * len(parts)),
        name="load",
    )(activations, after)


def term(mine_ref, other_ref, block):
    first = lax.rem(lax.axis_index("fsdp"), 2) == 0
    low, high = mine_ref[...], other_ref[...]
    whole = jnp.concatenate(
        [jnp.where(first, low, high), jnp.where(first, high, low)], axis=1
    )
    return jnp.dot(whole, block, preferred_element_type=jnp.float32).T


def low_held(held, mine, other, place, after):
    rank = mine.shape[0]
    _, tokens, rows = held.shape

    def kernel(mine_ref, other_ref, act_ref, after_ref, out_ref, token_ref):
        out_ref[...] = term(mine_ref, other_ref, act_ref[place]).astype(jnp.bfloat16)
        token_ref[...] = jnp.zeros_like(token_ref)

    return pl.pallas_call(
        kernel,
        in_specs=[pl.BlockSpec(memory_space=pltpu.VMEM)] * 3
        + [pl.BlockSpec(memory_space=pl.ANY)],
        out_specs=[pl.BlockSpec(memory_space=pltpu.VMEM)] * 2,
        out_shape=[jax.ShapeDtypeStruct((rows, rank), jnp.bfloat16), TOKEN],
        compiler_params=pltpu.CompilerParams(vmem_limit_bytes=VMEM),
        cost_estimate=cost(2 * tokens * rows * rank, 2 * tokens * rows),
        name="low_held",
    )(mine, other, held, after)


def low_rest(activations, mine, other, parts, kinds, after):
    rank = mine.shape[0]
    tokens, units = activations.shape
    rows = units // (lax.axis_size("dp") * CHUNKS)

    def kernel(mine_ref, other_ref, act_hbm, after_ref, *rest):
        held, sems = rest[-2:]
        copies = blocks_of(act_hbm, held, sems, parts, rows)
        for place, copy in enumerate(copies):
            copy.wait()
            rest[place][...] = term(mine_ref, other_ref, held[place]).astype(kinds[place])

    return pl.pallas_call(
        kernel,
        grid=(1,),
        in_specs=[pl.BlockSpec(memory_space=pltpu.VMEM)] * 2
        + [pl.BlockSpec(memory_space=pltpu.HBM), pl.BlockSpec(memory_space=pl.ANY)],
        out_specs=[pl.BlockSpec((rows, rank), lambda i: (0, 0))] * len(parts),
        out_shape=[pltpu.HBM((rows, rank), kind) for kind in kinds],
        scratch_shapes=[
            pltpu.VMEM((len(parts), tokens, rows), jnp.bfloat16),
            pltpu.SemaphoreType.DMA((len(parts),)),
        ],
        compiler_params=pltpu.CompilerParams(vmem_limit_bytes=WIDE),
        cost_estimate=cost(1000, 1000),
        name="low_rest",
    )(mine, other, activations, after)


def adam(own, near, far, first, second, chunk, before, after=()):
    rows, rank = own.shape
    tile = rows // 2
    first_fix = 1.0 - 0.9**STEP
    second_fix = 1.0 - 0.999**STEP

    def kernel(own_ref, near_ref, far_ref, first_ref, second_ref, *rest):
        normed_ref, first_out, second_out = rest[-3:]
        low = (
            own_ref[...]
            + near_ref[...].astype(jnp.float32)
            + far_ref[...].astype(jnp.float32)
        )
        first_next = 0.9 * first_ref[...] + 0.1 * low
        second_next = 0.999 * second_ref[...] + 0.001 * low * low
        first_out[...] = first_next
        second_out[...] = second_next
        normed_ref[...] = (
            first_next / first_fix / (jnp.sqrt(second_next / second_fix) + 1e-08)
        ).astype(jnp.bfloat16)

    local = pl.BlockSpec((tile, rank), lambda i: (i, 0))
    whole = pl.BlockSpec((tile, rank), lambda i: (chunk * 2 + i, 0))
    extra = [] if before is None else list(before)
    return pl.pallas_call(
        kernel,
        grid=(2,),
        in_specs=[local, local, local, whole, whole]
        + [pl.BlockSpec(memory_space=pl.ANY)] * (len(extra) + len(after)),
        out_specs=[local, whole, whole],
        out_shape=[
            jax.ShapeDtypeStruct((rows, rank), jnp.bfloat16),
            jax.ShapeDtypeStruct(first.shape, jnp.float32),
            jax.ShapeDtypeStruct(second.shape, jnp.float32),
        ],
        input_output_aliases={5: 1, 6: 2} if extra else {},
        compiler_params=pltpu.CompilerParams(vmem_limit_bytes=VMEM),
        cost_estimate=cost(30 * rows * rank, 24 * rows * rank),
        name="adam",
    )(own, near, far, first, second, *extra, *after)


def expand(place, normed, basis_cols, bit, chunk, shape, before):
    rows, rank = normed.shape
    width = basis_cols.shape[0]
    steps = 2
    tile = rows // steps

    def kernel(s, normed_ref, basis_ref, *rest):
        out_ref, token_ref = rest[-2:]
        product = lax.dot_general(
            normed_ref[...],
            basis_ref[...],
            (((1,), (1,)), ((), ())),
            preferred_element_type=jnp.float32,
        )
        out_ref[...] = (0.25 * product).astype(jnp.bfloat16)
        token_ref[...] = jnp.zeros_like(token_ref)

    extra = [] if before is None else [before]
    return pl.pallas_call(
        kernel,
        grid_spec=pltpu.PrefetchScalarGridSpec(
            num_scalar_prefetch=1,
            grid=(steps,),
            in_specs=[
                pl.BlockSpec((tile, rank), lambda i, s: (i, 0)),
                pl.BlockSpec((width, rank), lambda i, s: (0, 0)),
            ]
            + [pl.BlockSpec(memory_space=pl.ANY)] * len(extra),
            out_specs=[
                pl.BlockSpec(
                    (tile, width), lambda i, s: (((s[0] ^ bit) * CHUNKS + chunk) * steps + i, 0)
                ),
                pl.BlockSpec((8, 128), lambda i, s: (0, 0)),
            ],
        ),
        out_shape=[
            jax.ShapeDtypeStruct(shape, jnp.bfloat16),
            TOKEN,
        ],
        input_output_aliases={3: 0} if extra else {},
        compiler_params=pltpu.CompilerParams(vmem_limit_bytes=VMEM),
        cost_estimate=cost(60 * rows * rank * width, 60 * rows * width),
        name="expand",
    )(place, normed, basis_cols, *extra)


def paired(activations, out_grad, basis, first_moment, second_moment):
    f32, b16 = jnp.float32, jnp.bfloat16
    z = lax.axis_index("dp")
    width = basis.shape[0] // lax.axis_size("dp")
    fixed = functools.partial(pltpu.with_memory_space_constraint, memory_space=pltpu.HBM)
    shape = (activations.shape[1], width)
    basis_cols = lax.dynamic_slice_in_dim(basis, z * width, width, 0)

    give, keep = project(fixed(out_grad), fixed(basis))
    activations = fixed(activations)
    held, token = load(activations, ((3, 0), (1, 0)), keep)
    pair = keep + swap(give, "fsdp", 1)
    mine = settle(pair, swap(pair, "fsdp", 2), token)
    other = swap(mine, "fsdp", 1)

    cross_a, token = low_held(held, mine, other, 0, token)
    cross_a = swap(cross_a, "dp", 1)
    near_a, token = low_held(held, mine, other, 1, token)
    near_a = swap(near_a, "dp", 1)
    cross_b, two_a, own_a, two_b, near_b, own_b = low_rest(
        activations,
        mine,
        other,
        ((3, 1), (2, 0), (0, 0), (2, 1), (1, 1), (0, 1)),
        (b16, f32, f32, f32, b16, f32),
        token,
    )
    cross_b, near_b = swap(cross_b, "dp", 1), swap(near_b, "dp", 1)
    sum_a = swap((two_a + cross_a).astype(b16), "dp", 2)
    sum_b = swap((two_b + cross_b).astype(b16), "dp", 2)

    first_moment, second_moment = fixed(first_moment), fixed(second_moment)
    grow = functools.partial(expand, z[None])
    rows_a, *moments = adam(fixed(own_a), near_a, sum_a, first_moment, second_moment, 0, None)
    far_a = swap(rows_a, "dp", 2)
    next_a = swap(rows_a, "dp", 1)
    update, token = grow(rows_a, basis_cols, 0, 0, shape, None)
    rows_b, *moments = adam(
        fixed(own_b), near_b, sum_b, first_moment, second_moment, 1, moments, (token,)
    )
    far_b = swap(rows_b, "dp", 2)
    next_b = swap(rows_b, "dp", 1)
    last_a = swap(far_a, "dp", 1)
    update, token = grow(next_a, basis_cols, 1, 0, shape, update)
    update, token = grow(far_a, basis_cols, 2, 0, shape, update)
    update, token = grow(rows_b, basis_cols, 0, 1, shape, update)
    last_b = swap(far_b, "dp", 1)
    for bit, chunk, rows in ((3, 0, last_a), (1, 1, next_b), (2, 1, far_b), (3, 1, last_b)):
        update, token = grow(rows, basis_cols, bit, chunk, shape, update)
    return (update, *moments)


def general(activations, out_grad, basis, first_moment, second_moment):
    features = out_grad.shape[1]
    fsdp_index = lax.axis_index("fsdp")
    basis_rows = lax.dynamic_slice_in_dim(basis, fsdp_index * features, features, 0)
    partial_proj = jnp.dot(out_grad, basis_rows, preferred_element_type=jnp.float32)
    projected = lax.psum(partial_proj, "fsdp").astype(jnp.bfloat16)
    low_grad = lax.psum_scatter(
        lax.dot_general(
            activations, projected, (((0,), (0,)), ((), ())), preferred_element_type=jnp.float32
        ),
        "dp",
        scatter_dimension=0,
        tiled=True,
    )
    first_next = 0.9 * first_moment + 0.1 * low_grad
    second_next = 0.999 * second_moment + 0.001 * low_grad * low_grad
    first_fix = 1.0 - 0.9**STEP
    second_fix = 1.0 - 0.999**STEP
    normed = (first_next / first_fix / (jnp.sqrt(second_next / second_fix) + 1e-08)).astype(
        jnp.bfloat16
    )
    width = basis.shape[0] // lax.axis_size("dp")
    basis_cols = lax.dynamic_slice_in_dim(basis, lax.axis_index("dp") * width, width, 0)
    product = lax.dot_general(
        lax.all_gather(normed, "dp", axis=0, tiled=True),
        basis_cols,
        (((1,), (1,)), ((), ())),
        preferred_element_type=jnp.float32,
    )
    update = (0.25 * product).astype(jnp.bfloat16)
    return (update, first_next, second_next)


def solution(mesh):
    placed = (
        P(("groups", "dp"), "fsdp"),
        P(("groups", "dp"), "fsdp"),
        P("groups", None),
        P(("groups", "fsdp", "dp"), None),
        P(("groups", "fsdp", "dp"), None),
    )
    on_device = paired if mesh.shape["dp"] == 4 and mesh.shape["fsdp"] == 4 else general
    return jax.shard_map(
        on_device,
        mesh=mesh,
        in_specs=placed,
        out_specs=(
            P(("groups", "fsdp"), "dp"),
            P(("groups", "fsdp", "dp"), None),
            P(("groups", "fsdp", "dp"), None),
        ),
        check_vma=False,
    )
```

```python
import functools

import jax
import jax.numpy as jnp
from jax import lax
from jax.experimental import pallas as pl
from jax.experimental.pallas import tpu as pltpu
from jax.sharding import PartitionSpec as P

STEP = 10
CHUNKS = 2
VMEM = 16 << 20
WIDE = 32 << 20
PIECES = 3
TOKEN = jax.ShapeDtypeStruct((8, 128), jnp.float32)


def cost(flops, moved):
    return pl.CostEstimate(flops=flops, bytes_accessed=moved, transcendentals=0)


def swap(value, axis, bit):
    n = lax.axis_size(axis)
    return lax.ppermute(value, axis, [(i, i ^ bit) for i in range(n)])


def project(out_grad, basis, turn, after=()):
    tokens, features = out_grad.shape
    rows, rank = tokens // 2, basis.shape[1]
    piece = rows // PIECES

    def kernel(grad_hbm, basis_hbm, *rest):
        out_ref, grad, base, sems = rest[-4:]
        place = lax.axis_index("fsdp")
        half = lax.rem(place + 1 + turn, 2)
        copies = [
            pltpu.make_async_copy(
                basis_hbm.at[pl.ds(pl.multiple_of(place * features, features), features), :],
                base,
                sems.at[0],
            )
        ]
        for part in range(PIECES):
            first = half * rows + part * piece
            copies.append(
                pltpu.make_async_copy(
                    grad_hbm.at[pl.ds(pl.multiple_of(first, piece), piece), :],
                    grad.at[pl.ds(part * piece, piece), :],
                    sems.at[part + 1],
                )
            )
        for copy in copies:
            copy.start()
        for copy in copies:
            copy.wait()
        out_ref[...] = jnp.dot(
            grad[...], base[...], preferred_element_type=jnp.float32
        ).T

    return pl.pallas_call(
        kernel,
        in_specs=[pl.BlockSpec(memory_space=pltpu.HBM)] * 2
        + [pl.BlockSpec(memory_space=pl.ANY)] * len(after),
        out_specs=pl.BlockSpec(memory_space=pltpu.VMEM),
        out_shape=jax.ShapeDtypeStruct((rank, rows), jnp.float32),
        scratch_shapes=[
            pltpu.VMEM((rows, features), jnp.bfloat16),
            pltpu.VMEM((features, rank), jnp.bfloat16),
            pltpu.SemaphoreType.DMA((PIECES + 1,)),
        ],
        compiler_params=pltpu.CompilerParams(vmem_limit_bytes=VMEM),
        cost_estimate=cost(1000, 1000),
        name="project",
    )(out_grad, basis, *after)


def settle(pair, far, after):
    def kernel(pair_ref, far_ref, after_ref, out_ref):
        out_ref[...] = (pair_ref[...] + far_ref[...]).astype(jnp.bfloat16)

    return pl.pallas_call(
        kernel,
        in_specs=[pl.BlockSpec(memory_space=pltpu.VMEM)] * 2
        + [pl.BlockSpec(memory_space=pl.ANY)],
        out_specs=pl.BlockSpec(memory_space=pltpu.VMEM),
        out_shape=jax.ShapeDtypeStruct(pair.shape, jnp.bfloat16),
        compiler_params=pltpu.CompilerParams(vmem_limit_bytes=VMEM),
        cost_estimate=cost(pair.size, 10 * pair.size),
        name="settle",
    )(pair, far, after)


def merge(own, got, waiting):
    def kernel(own_ref, got_ref, waiting_ref, out_ref, next_ref):
        out_ref[...] = (own_ref[...] + got_ref[...].astype(jnp.float32)).astype(jnp.bfloat16)
        next_ref[...] = waiting_ref[...]

    return pl.pallas_call(
        kernel,
        in_specs=[pl.BlockSpec(memory_space=pltpu.VMEM)] * 3,
        out_specs=[pl.BlockSpec(memory_space=pltpu.VMEM)] * 2,
        out_shape=[
            jax.ShapeDtypeStruct(got.shape, jnp.bfloat16),
            jax.ShapeDtypeStruct(waiting.shape, jnp.bfloat16),
        ],
        compiler_params=pltpu.CompilerParams(vmem_limit_bytes=VMEM),
        cost_estimate=cost(own.size, 8 * own.size),
        name="merge",
    )(own, got, waiting)


def pass_on(value, after):
    def kernel(value_ref, after_ref, out_ref):
        out_ref[...] = value_ref[...]

    return pl.pallas_call(
        kernel,
        in_specs=[pl.BlockSpec(memory_space=pltpu.VMEM), pl.BlockSpec(memory_space=pl.ANY)],
        out_specs=pl.BlockSpec(memory_space=pltpu.VMEM),
        out_shape=jax.ShapeDtypeStruct(value.shape, value.dtype),
        compiler_params=pltpu.CompilerParams(vmem_limit_bytes=VMEM),
        cost_estimate=cost(0, 4 * value.size),
        name="pass_on",
    )(value, after)


def blocks_of(act_hbm, held, sems, parts, rows):
    copies = []
    for place, (bit, chunk) in enumerate(parts):
        block = (lax.axis_index("dp") ^ bit) * CHUNKS + chunk
        copies.append(
            pltpu.make_async_copy(
                act_hbm.at[:, pl.ds(pl.multiple_of(block * rows, 128), rows)],
                held.at[place],
                sems.at[place],
            )
        )
    for copy in copies:
        copy.start()
    return copies


def load(activations, basis, parts, after):
    tokens, units = activations.shape
    rows = units // (lax.axis_size("dp") * CHUNKS)
    width, rank = basis.shape[0] // lax.axis_size("dp"), basis.shape[1]

    def kernel(act_hbm, basis_hbm, after_ref, held, columns, token_ref, sems):
        first = pl.multiple_of(lax.axis_index("dp") * width, width)
        extra = pltpu.make_async_copy(
            basis_hbm.at[pl.ds(first, width), :], columns, sems.at[len(parts)]
        )
        extra.start()
        for copy in blocks_of(act_hbm, held, sems, parts, rows):
            copy.wait()
        extra.wait()
        token_ref[...] = jnp.zeros_like(token_ref)

    return pl.pallas_call(
        kernel,
        in_specs=[pl.BlockSpec(memory_space=pltpu.HBM)] * 2 + [pl.BlockSpec(memory_space=pl.ANY)],
        out_specs=[pl.BlockSpec(memory_space=pltpu.VMEM)] * 3,
        out_shape=[
            jax.ShapeDtypeStruct((len(parts), tokens, rows), jnp.bfloat16),
            jax.ShapeDtypeStruct((width, rank), jnp.bfloat16),
            TOKEN,
        ],
        scratch_shapes=[pltpu.SemaphoreType.DMA((len(parts) + 1,))],
        compiler_params=pltpu.CompilerParams(vmem_limit_bytes=VMEM),
        cost_estimate=cost(0, 2 * tokens * rows * len(parts)),
        name="load",
    )(activations, basis, after)


def term(mine_ref, other_ref, block):
    first = lax.rem(lax.axis_index("fsdp"), 2) == 0
    low, high = mine_ref[...], other_ref[...]
    whole = jnp.concatenate(
        [jnp.where(first, low, high), jnp.where(first, high, low)], axis=1
    )
    return jnp.dot(whole, block, preferred_element_type=jnp.float32).T


def low_held(held, mine, other, place, after):
    rank = mine.shape[0]
    _, tokens, rows = held.shape

    def kernel(mine_ref, other_ref, act_ref, after_ref, out_ref, token_ref):
        out_ref[...] = term(mine_ref, other_ref, act_ref[place]).astype(jnp.bfloat16)
        token_ref[...] = jnp.zeros_like(token_ref)

    return pl.pallas_call(
        kernel,
        in_specs=[pl.BlockSpec(memory_space=pltpu.VMEM)] * 3
        + [pl.BlockSpec(memory_space=pl.ANY)],
        out_specs=[pl.BlockSpec(memory_space=pltpu.VMEM)] * 2,
        out_shape=[jax.ShapeDtypeStruct((rows, rank), jnp.bfloat16), TOKEN],
        compiler_params=pltpu.CompilerParams(vmem_limit_bytes=VMEM),
        cost_estimate=cost(2 * tokens * rows * rank, 2 * tokens * rows),
        name="low_held",
    )(mine, other, held, after)


def low_rest(activations, mine, other, groups, after):
    rank = mine.shape[0]
    tokens, units = activations.shape
    rows = units // (lax.axis_size("dp") * CHUNKS)
    parts = [part for _, _, blocks in groups for part in blocks]

    def kernel(mine_ref, other_ref, act_hbm, after_ref, *rest):
        held, sems = rest[-2:]
        copies = blocks_of(act_hbm, held, sems, parts, rows)
        place = 0
        for out_ref, (kind, _, blocks) in zip(rest, groups):
            for row in range(len(blocks)):
                copies[place].wait()
                out_ref[row * rows : (row + 1) * rows, :] = term(
                    mine_ref, other_ref, held[place]
                ).astype(kind)
                place += 1

    shapes = [(len(blocks) * rows, rank) for _, _, blocks in groups]
    return pl.pallas_call(
        kernel,
        grid=(1,),
        in_specs=[pl.BlockSpec(memory_space=pltpu.VMEM)] * 2
        + [pl.BlockSpec(memory_space=pltpu.HBM), pl.BlockSpec(memory_space=pl.ANY)],
        out_specs=[pl.BlockSpec(shape, lambda i: (0, 0)) for shape in shapes],
        out_shape=[memory(shape, kind) for shape, (kind, memory, _) in zip(shapes, groups)],
        scratch_shapes=[
            pltpu.VMEM((len(parts), tokens, rows), jnp.bfloat16),
            pltpu.SemaphoreType.DMA((len(parts),)),
        ],
        compiler_params=pltpu.CompilerParams(vmem_limit_bytes=WIDE),
        cost_estimate=cost(1000, 1000),
        name="low_rest",
    )(mine, other, activations, after)


def adam(own, near, far, first, second, chunk, before, after=()):
    rows, rank = far.shape
    tile = rows // 2
    first_fix = 1.0 - 0.9**STEP
    second_fix = 1.0 - 0.999**STEP

    def kernel(own_ref, near_ref, far_ref, first_ref, second_ref, *rest):
        normed_ref, first_out, second_out = rest[-3:]
        low = (
            own_ref[...]
            + near_ref[...].astype(jnp.float32)
            + far_ref[...].astype(jnp.float32)
        )
        first_next = 0.9 * first_ref[...] + 0.1 * low
        second_next = 0.999 * second_ref[...] + 0.001 * low * low
        first_out[...] = first_next
        second_out[...] = second_next
        normed_ref[...] = (
            first_next / first_fix / (jnp.sqrt(second_next / second_fix) + 1e-08)
        ).astype(jnp.bfloat16)

    local = pl.BlockSpec((tile, rank), lambda i: (i, 0))
    whole = pl.BlockSpec((tile, rank), lambda i: (chunk * 2 + i, 0))
    extra = [] if before is None else list(before)
    return pl.pallas_call(
        kernel,
        grid=(2,),
        in_specs=[whole, local, local, whole, whole]
        + [pl.BlockSpec(memory_space=pl.ANY)] * (len(extra) + len(after)),
        out_specs=[local, whole, whole],
        out_shape=[
            jax.ShapeDtypeStruct((rows, rank), jnp.bfloat16),
            jax.ShapeDtypeStruct(first.shape, jnp.float32),
            jax.ShapeDtypeStruct(second.shape, jnp.float32),
        ],
        input_output_aliases={5: 1, 6: 2} if extra else {},
        compiler_params=pltpu.CompilerParams(vmem_limit_bytes=VMEM),
        cost_estimate=cost(30 * rows * rank, 24 * rows * rank),
        name="adam",
    )(own, near, far, first, second, *extra, *after)


def expand(place, basis_cols, shape, before, pieces):
    rows, rank = pieces[0][0].shape
    width = basis_cols.shape[0]
    steps = 2
    tile = rows // steps
    count = len(pieces)

    def block(i, s):
        place = jnp.int32(0)
        for turn, (_, bit, chunk) in enumerate(pieces):
            here = ((s[0] ^ bit) * CHUNKS + chunk) * steps + i - turn * steps
            place = here if turn == 0 else jnp.where(i >= turn * steps, here, place)
        return place, 0

    def kernel(s, basis_ref, *rest):
        out_ref, token_ref = rest[-2:]
        step = pl.program_id(0)
        for turn in range(count):

            @pl.when(step // steps == turn)
            def _():
                product = lax.dot_general(
                    rest[turn][...],
                    basis_ref[...],
                    (((1,), (1,)), ((), ())),
                    preferred_element_type=jnp.float32,
                )
                out_ref[...] = (0.25 * product).astype(jnp.bfloat16)

        token_ref[...] = jnp.zeros_like(token_ref)

    def rows_of(turn):
        return lambda i, s: (jnp.clip(i - turn * steps, 0, steps - 1), 0)

    extra = [] if before is None else [before]
    return pl.pallas_call(
        kernel,
        grid_spec=pltpu.PrefetchScalarGridSpec(
            num_scalar_prefetch=1,
            grid=(count * steps,),
            in_specs=[pl.BlockSpec((width, rank), lambda i, s: (0, 0))]
            + [pl.BlockSpec((tile, rank), rows_of(turn)) for turn in range(count)]
            + [pl.BlockSpec(memory_space=pl.ANY)] * len(extra),
            out_specs=[
                pl.BlockSpec((tile, width), block),
                pl.BlockSpec((8, 128), lambda i, s: (0, 0)),
            ],
        ),
        out_shape=[jax.ShapeDtypeStruct(shape, jnp.bfloat16), TOKEN],
        input_output_aliases={2 + count: 0} if extra else {},
        compiler_params=pltpu.CompilerParams(vmem_limit_bytes=VMEM),
        cost_estimate=cost(60 * rows * rank * width * count, 60 * rows * width * count),
        name="expand",
    )(place, basis_cols, *[piece for piece, _, _ in pieces], *extra)


def paired(activations, out_grad, basis, first_moment, second_moment):
    f32, b16 = jnp.float32, jnp.bfloat16
    z = lax.axis_index("dp")
    width = basis.shape[0] // lax.axis_size("dp")
    fixed = functools.partial(pltpu.with_memory_space_constraint, memory_space=pltpu.HBM)
    shape = (activations.shape[1], width)
    out_grad, activations, basis = fixed(out_grad), fixed(activations), fixed(basis)
    give = project(out_grad, basis, 0)
    keep = project(out_grad, basis, 1, (give,))
    held, basis_cols, token = load(activations, basis, ((3, 0), (3, 1)), keep)
    pair = keep + swap(give, "fsdp", 1)
    mine = settle(pair, swap(pair, "fsdp", 2), token)
    other = swap(mine, "fsdp", 1)

    cross_a, token = low_held(held, mine, other, 0, token)
    cross_a = swap(cross_a, "dp", 1)
    cross_b, token = low_held(held, mine, other, 1, token)
    cross_b = swap(cross_b, "dp", 1)
    plain = jax.ShapeDtypeStruct
    two_a, near_a, two_b, near_b, own = low_rest(
        activations,
        mine,
        other,
        (
            (f32, plain, ((2, 0),)),
            (b16, plain, ((1, 0),)),
            (f32, plain, ((2, 1),)),
            (b16, plain, ((1, 1),)),
            (f32, pltpu.HBM, ((0, 0), (0, 1))),
        ),
        token,
    )
    sum_a, near_a = merge(two_a, cross_a, near_a)
    sum_a = swap(sum_a, "dp", 2)
    near_a = swap(near_a, "dp", 1)
    sum_b, near_b = merge(two_b, cross_b, near_b)
    sum_b = swap(sum_b, "dp", 2)
    near_b = swap(near_b, "dp", 1)

    first_moment, second_moment, own = fixed(first_moment), fixed(second_moment), fixed(own)
    grow = functools.partial(expand, z[None], basis_cols, shape)
    rows_a, *moments = adam(own, near_a, sum_a, first_moment, second_moment, 0, None)
    far_a = swap(rows_a, "dp", 2)
    next_a = swap(rows_a, "dp", 1)
    update, token = grow(None, ((rows_a, 0, 0),))
    rows_b, *moments = adam(
        own, near_b, sum_b, first_moment, second_moment, 1, moments, (token,)
    )
    far_b = swap(rows_b, "dp", 2)
    next_b = swap(rows_b, "dp", 1)
    update, token = grow(update, ((next_a, 1, 0),))
    last_a = swap(pass_on(far_a, token), "dp", 1)
    update, token = grow(update, ((far_a, 2, 0), (rows_b, 0, 1)))
    last_b = swap(pass_on(far_b, token), "dp", 1)
    for pieces in (
        ((next_b, 1, 1), (far_b, 2, 1)),
        ((last_a, 3, 0), (last_b, 3, 1)),
    ):
        update, token = grow(update, pieces)
    return (update, *moments)


def general(activations, out_grad, basis, first_moment, second_moment):
    features = out_grad.shape[1]
    fsdp_index = lax.axis_index("fsdp")
    basis_rows = lax.dynamic_slice_in_dim(basis, fsdp_index * features, features, 0)
    partial_proj = jnp.dot(out_grad, basis_rows, preferred_element_type=jnp.float32)
    projected = lax.psum(partial_proj, "fsdp").astype(jnp.bfloat16)
    low_grad = lax.psum_scatter(
        lax.dot_general(
            activations, projected, (((0,), (0,)), ((), ())), preferred_element_type=jnp.float32
        ),
        "dp",
        scatter_dimension=0,
        tiled=True,
    )
    first_next = 0.9 * first_moment + 0.1 * low_grad
    second_next = 0.999 * second_moment + 0.001 * low_grad * low_grad
    first_fix = 1.0 - 0.9**STEP
    second_fix = 1.0 - 0.999**STEP
    normed = (first_next / first_fix / (jnp.sqrt(second_next / second_fix) + 1e-08)).astype(
        jnp.bfloat16
    )
    width = basis.shape[0] // lax.axis_size("dp")
    basis_cols = lax.dynamic_slice_in_dim(basis, lax.axis_index("dp") * width, width, 0)
    product = lax.dot_general(
        lax.all_gather(normed, "dp", axis=0, tiled=True),
        basis_cols,
        (((1,), (1,)), ((), ())),
        preferred_element_type=jnp.float32,
    )
    update = (0.25 * product).astype(jnp.bfloat16)
    return (update, first_next, second_next)


def solution(mesh):
    placed = (
        P(("groups", "dp"), "fsdp"),
        P(("groups", "dp"), "fsdp"),
        P("groups", None),
        P(("groups", "fsdp", "dp"), None),
        P(("groups", "fsdp", "dp"), None),
    )
    on_device = paired if mesh.shape["dp"] == 4 and mesh.shape["fsdp"] == 4 else general
    return jax.shard_map(
        on_device,
        mesh=mesh,
        in_specs=placed,
        out_specs=(
            P(("groups", "fsdp"), "dp"),
            P(("groups", "fsdp", "dp"), None),
            P(("groups", "fsdp", "dp"), None),
        ),
        check_vma=False,
    )
```

```python
import functools

import jax
import jax.numpy as jnp
from jax import lax
from jax.experimental import pallas as pl
from jax.experimental.pallas import tpu as pltpu
from jax.sharding import PartitionSpec as P

STEP = 10
CHUNKS = 2
VMEM = 16 << 20
WIDE = 32 << 20
PIECES = 3
TOKEN = jax.ShapeDtypeStruct((8, 128), jnp.float32)


def cost(flops, moved):
    return pl.CostEstimate(flops=flops, bytes_accessed=moved, transcendentals=0)


def swap(value, axis, bit):
    n = lax.axis_size(axis)
    return lax.ppermute(value, axis, [(i, i ^ bit) for i in range(n)])


def project_give(out_grad, basis):
    tokens, features = out_grad.shape
    rows, rank = tokens // 2, basis.shape[1]
    piece = rows // PIECES

    def kernel(grad_hbm, basis_hbm, out_ref, held, base, grad, sems):
        place = lax.axis_index("fsdp")
        core = lax.rem(place, 2)
        copies = [
            pltpu.make_async_copy(
                basis_hbm.at[pl.ds(pl.multiple_of(place * features, features), features), :],
                base,
                sems.at[0],
            )
        ]
        for turn, (half, target) in enumerate(((1 - core, grad), (core, held))):
            for part in range(PIECES):
                first = half * rows + part * piece
                copies.append(
                    pltpu.make_async_copy(
                        grad_hbm.at[pl.ds(pl.multiple_of(first, piece), piece), :],
                        target.at[pl.ds(part * piece, piece), :],
                        sems.at[turn * PIECES + part + 1],
                    )
                )
        for copy in copies:
            copy.start()
        for copy in copies[: PIECES + 1]:
            copy.wait()
        out_ref[...] = jnp.dot(
            grad[...], base[...], preferred_element_type=jnp.float32
        ).T
        for copy in copies[PIECES + 1 :]:
            copy.wait()

    return pl.pallas_call(
        kernel,
        in_specs=[pl.BlockSpec(memory_space=pltpu.HBM)] * 2,
        out_specs=[pl.BlockSpec(memory_space=pltpu.VMEM)] * 3,
        out_shape=[
            jax.ShapeDtypeStruct((rank, rows), jnp.float32),
            jax.ShapeDtypeStruct((rows, features), jnp.bfloat16),
            jax.ShapeDtypeStruct((features, rank), jnp.bfloat16),
        ],
        scratch_shapes=[
            pltpu.VMEM((rows, features), jnp.bfloat16),
            pltpu.SemaphoreType.DMA((2 * PIECES + 1,)),
        ],
        compiler_params=pltpu.CompilerParams(vmem_limit_bytes=VMEM),
        cost_estimate=cost(1000, 1000),
        name="project_give",
    )(out_grad, basis)


def project_keep(grad, base):
    rows, rank = grad.shape[0], base.shape[1]

    def kernel(grad_ref, base_ref, out_ref):
        out_ref[...] = jnp.dot(
            grad_ref[...], base_ref[...], preferred_element_type=jnp.float32
        ).T

    return pl.pallas_call(
        kernel,
        in_specs=[pl.BlockSpec(memory_space=pltpu.VMEM)] * 2,
        out_specs=pl.BlockSpec(memory_space=pltpu.VMEM),
        out_shape=jax.ShapeDtypeStruct((rank, rows), jnp.float32),
        compiler_params=pltpu.CompilerParams(vmem_limit_bytes=VMEM),
        cost_estimate=cost(1000, 1000),
        name="project_keep",
    )(grad, base)


def settle(pair, far, after):
    def kernel(pair_ref, far_ref, after_ref, out_ref):
        out_ref[...] = (pair_ref[...] + far_ref[...]).astype(jnp.bfloat16)

    return pl.pallas_call(
        kernel,
        in_specs=[pl.BlockSpec(memory_space=pltpu.VMEM)] * 2
        + [pl.BlockSpec(memory_space=pl.ANY)],
        out_specs=pl.BlockSpec(memory_space=pltpu.VMEM),
        out_shape=jax.ShapeDtypeStruct(pair.shape, jnp.bfloat16),
        compiler_params=pltpu.CompilerParams(vmem_limit_bytes=VMEM),
        cost_estimate=cost(pair.size, 10 * pair.size),
        name="settle",
    )(pair, far, after)


def merge(own, got, waiting):
    def kernel(own_ref, got_ref, waiting_ref, out_ref, next_ref):
        out_ref[...] = (own_ref[...] + got_ref[...].astype(jnp.float32)).astype(jnp.bfloat16)
        next_ref[...] = waiting_ref[...]

    return pl.pallas_call(
        kernel,
        in_specs=[pl.BlockSpec(memory_space=pltpu.VMEM)] * 3,
        out_specs=[pl.BlockSpec(memory_space=pltpu.VMEM)] * 2,
        out_shape=[
            jax.ShapeDtypeStruct(got.shape, jnp.bfloat16),
            jax.ShapeDtypeStruct(waiting.shape, jnp.bfloat16),
        ],
        compiler_params=pltpu.CompilerParams(vmem_limit_bytes=VMEM),
        cost_estimate=cost(own.size, 8 * own.size),
        name="merge",
    )(own, got, waiting)


def pass_on(value, after):
    def kernel(value_ref, after_ref, out_ref):
        out_ref[...] = value_ref[...]

    return pl.pallas_call(
        kernel,
        in_specs=[pl.BlockSpec(memory_space=pltpu.VMEM), pl.BlockSpec(memory_space=pl.ANY)],
        out_specs=pl.BlockSpec(memory_space=pltpu.VMEM),
        out_shape=jax.ShapeDtypeStruct(value.shape, value.dtype),
        compiler_params=pltpu.CompilerParams(vmem_limit_bytes=VMEM),
        cost_estimate=cost(0, 4 * value.size),
        name="pass_on",
    )(value, after)


def blocks_of(act_hbm, held, sems, parts, rows):
    copies = []
    for place, (bit, chunk) in enumerate(parts):
        block = (lax.axis_index("dp") ^ bit) * CHUNKS + chunk
        copies.append(
            pltpu.make_async_copy(
                act_hbm.at[:, pl.ds(pl.multiple_of(block * rows, 128), rows)],
                held.at[place],
                sems.at[place],
            )
        )
    for copy in copies:
        copy.start()
    return copies


def load(activations, basis, parts, after):
    tokens, units = activations.shape
    rows = units // (lax.axis_size("dp") * CHUNKS)
    width, rank = basis.shape[0] // lax.axis_size("dp"), basis.shape[1]

    def kernel(act_hbm, basis_hbm, after_ref, held, columns, token_ref, sems):
        first = pl.multiple_of(lax.axis_index("dp") * width, width)
        extra = pltpu.make_async_copy(
            basis_hbm.at[pl.ds(first, width), :], columns, sems.at[len(parts)]
        )
        extra.start()
        for copy in blocks_of(act_hbm, held, sems, parts, rows):
            copy.wait()
        extra.wait()
        token_ref[...] = jnp.zeros_like(token_ref)

    return pl.pallas_call(
        kernel,
        in_specs=[pl.BlockSpec(memory_space=pltpu.HBM)] * 2 + [pl.BlockSpec(memory_space=pl.ANY)],
        out_specs=[pl.BlockSpec(memory_space=pltpu.VMEM)] * 3,
        out_shape=[
            jax.ShapeDtypeStruct((len(parts), tokens, rows), jnp.bfloat16),
            jax.ShapeDtypeStruct((width, rank), jnp.bfloat16),
            TOKEN,
        ],
        scratch_shapes=[pltpu.SemaphoreType.DMA((len(parts) + 1,))],
        compiler_params=pltpu.CompilerParams(vmem_limit_bytes=VMEM),
        cost_estimate=cost(0, 2 * tokens * rows * len(parts)),
        name="load",
    )(activations, basis, after)


def term(mine_ref, other_ref, block):
    first = lax.rem(lax.axis_index("fsdp"), 2) == 0
    low, high = mine_ref[...], other_ref[...]
    whole = jnp.concatenate(
        [jnp.where(first, low, high), jnp.where(first, high, low)], axis=1
    )
    return jnp.dot(whole, block, preferred_element_type=jnp.float32).T


def low_held(held, mine, other, place, after):
    rank = mine.shape[0]
    _, tokens, rows = held.shape

    def kernel(mine_ref, other_ref, act_ref, after_ref, out_ref, token_ref):
        out_ref[...] = term(mine_ref, other_ref, act_ref[place]).astype(jnp.bfloat16)
        token_ref[...] = jnp.zeros_like(token_ref)

    return pl.pallas_call(
        kernel,
        in_specs=[pl.BlockSpec(memory_space=pltpu.VMEM)] * 3
        + [pl.BlockSpec(memory_space=pl.ANY)],
        out_specs=[pl.BlockSpec(memory_space=pltpu.VMEM)] * 2,
        out_shape=[jax.ShapeDtypeStruct((rows, rank), jnp.bfloat16), TOKEN],
        compiler_params=pltpu.CompilerParams(vmem_limit_bytes=VMEM),
        cost_estimate=cost(2 * tokens * rows * rank, 2 * tokens * rows),
        name="low_held",
    )(mine, other, held, after)


def low_rest(activations, mine, other, groups, after):
    rank = mine.shape[0]
    tokens, units = activations.shape
    rows = units // (lax.axis_size("dp") * CHUNKS)
    parts = [part for _, _, blocks in groups for part in blocks]

    def kernel(mine_ref, other_ref, act_hbm, after_ref, *rest):
        held, sems = rest[-2:]
        copies = blocks_of(act_hbm, held, sems, parts, rows)
        place = 0
        for out_ref, (kind, _, blocks) in zip(rest, groups):
            for row in range(len(blocks)):
                copies[place].wait()
                out_ref[row * rows : (row + 1) * rows, :] = term(
                    mine_ref, other_ref, held[place]
                ).astype(kind)
                place += 1

    shapes = [(len(blocks) * rows, rank) for _, _, blocks in groups]
    return pl.pallas_call(
        kernel,
        grid=(1,),
        in_specs=[pl.BlockSpec(memory_space=pltpu.VMEM)] * 2
        + [pl.BlockSpec(memory_space=pltpu.HBM), pl.BlockSpec(memory_space=pl.ANY)],
        out_specs=[pl.BlockSpec(shape, lambda i: (0, 0)) for shape in shapes],
        out_shape=[memory(shape, kind) for shape, (kind, memory, _) in zip(shapes, groups)],
        scratch_shapes=[
            pltpu.VMEM((len(parts), tokens, rows), jnp.bfloat16),
            pltpu.SemaphoreType.DMA((len(parts),)),
        ],
        compiler_params=pltpu.CompilerParams(vmem_limit_bytes=WIDE),
        cost_estimate=cost(1000, 1000),
        name="low_rest",
    )(mine, other, activations, after)


def adam(own, near, far, first, second, chunk, before, after=()):
    rows, rank = far.shape
    tile = rows // 2
    first_fix = 1.0 - 0.9**STEP
    second_fix = 1.0 - 0.999**STEP

    def kernel(own_ref, near_ref, far_ref, first_ref, second_ref, *rest):
        normed_ref, first_out, second_out = rest[-3:]
        low = (
            own_ref[...]
            + near_ref[...].astype(jnp.float32)
            + far_ref[...].astype(jnp.float32)
        )
        first_next = 0.9 * first_ref[...] + 0.1 * low
        second_next = 0.999 * second_ref[...] + 0.001 * low * low
        first_out[...] = first_next
        second_out[...] = second_next
        normed_ref[...] = (
            first_next / first_fix / (jnp.sqrt(second_next / second_fix) + 1e-08)
        ).astype(jnp.bfloat16)

    local = pl.BlockSpec((tile, rank), lambda i: (i, 0))
    whole = pl.BlockSpec((tile, rank), lambda i: (chunk * 2 + i, 0))
    extra = [] if before is None else list(before)
    return pl.pallas_call(
        kernel,
        grid=(2,),
        in_specs=[whole, local, local, whole, whole]
        + [pl.BlockSpec(memory_space=pl.ANY)] * (len(extra) + len(after)),
        out_specs=[local, whole, whole],
        out_shape=[
            jax.ShapeDtypeStruct((rows, rank), jnp.bfloat16),
            jax.ShapeDtypeStruct(first.shape, jnp.float32),
            jax.ShapeDtypeStruct(second.shape, jnp.float32),
        ],
        input_output_aliases={5: 1, 6: 2} if extra else {},
        compiler_params=pltpu.CompilerParams(vmem_limit_bytes=VMEM),
        cost_estimate=cost(30 * rows * rank, 24 * rows * rank),
        name="adam",
    )(own, near, far, first, second, *extra, *after)


def expand(place, basis_cols, shape, before, pieces):
    rows, rank = pieces[0][0].shape
    width = basis_cols.shape[0]
    steps = 2
    tile = rows // steps
    count = len(pieces)

    def block(i, s):
        place = jnp.int32(0)
        for turn, (_, bit, chunk) in enumerate(pieces):
            here = ((s[0] ^ bit) * CHUNKS + chunk) * steps + i - turn * steps
            place = here if turn == 0 else jnp.where(i >= turn * steps, here, place)
        return place, 0

    def kernel(s, basis_ref, *rest):
        out_ref, token_ref = rest[-2:]
        step = pl.program_id(0)
        for turn in range(count):

            @pl.when(step // steps == turn)
            def _():
                product = lax.dot_general(
                    rest[turn][...],
                    basis_ref[...],
                    (((1,), (1,)), ((), ())),
                    preferred_element_type=jnp.float32,
                )
                out_ref[...] = (0.25 * product).astype(jnp.bfloat16)

        token_ref[...] = jnp.zeros_like(token_ref)

    def rows_of(turn):
        return lambda i, s: (jnp.clip(i - turn * steps, 0, steps - 1), 0)

    extra = [] if before is None else [before]
    return pl.pallas_call(
        kernel,
        grid_spec=pltpu.PrefetchScalarGridSpec(
            num_scalar_prefetch=1,
            grid=(count * steps,),
            in_specs=[pl.BlockSpec((width, rank), lambda i, s: (0, 0))]
            + [pl.BlockSpec((tile, rank), rows_of(turn)) for turn in range(count)]
            + [pl.BlockSpec(memory_space=pl.ANY)] * len(extra),
            out_specs=[
                pl.BlockSpec((tile, width), block),
                pl.BlockSpec((8, 128), lambda i, s: (0, 0)),
            ],
        ),
        out_shape=[jax.ShapeDtypeStruct(shape, jnp.bfloat16), TOKEN],
        input_output_aliases={2 + count: 0} if extra else {},
        compiler_params=pltpu.CompilerParams(vmem_limit_bytes=VMEM),
        cost_estimate=cost(60 * rows * rank * width * count, 60 * rows * width * count),
        name="expand",
    )(place, basis_cols, *[piece for piece, _, _ in pieces], *extra)


def paired(activations, out_grad, basis, first_moment, second_moment):
    f32, b16 = jnp.float32, jnp.bfloat16
    z = lax.axis_index("dp")
    width = basis.shape[0] // lax.axis_size("dp")
    fixed = functools.partial(pltpu.with_memory_space_constraint, memory_space=pltpu.HBM)
    shape = (activations.shape[1], width)
    out_grad, activations, basis = fixed(out_grad), fixed(activations), fixed(basis)
    give, grad, base = project_give(out_grad, basis)
    keep = project_keep(grad, base)
    held, basis_cols, token = load(activations, basis, ((3, 0), (3, 1)), keep)
    pair = keep + swap(give, "fsdp", 1)
    mine = settle(pair, swap(pair, "fsdp", 2), token)
    other = swap(mine, "fsdp", 1)

    cross_a, token = low_held(held, mine, other, 0, token)
    cross_a = swap(cross_a, "dp", 1)
    cross_b, token = low_held(held, mine, other, 1, token)
    cross_b = swap(cross_b, "dp", 1)
    plain = jax.ShapeDtypeStruct
    two_a, near_a, two_b, near_b, own = low_rest(
        activations,
        mine,
        other,
        (
            (f32, plain, ((2, 0),)),
            (b16, plain, ((1, 0),)),
            (f32, plain, ((2, 1),)),
            (b16, plain, ((1, 1),)),
            (f32, pltpu.HBM, ((0, 0), (0, 1))),
        ),
        token,
    )
    sum_a, near_a = merge(two_a, cross_a, near_a)
    sum_a = swap(sum_a, "dp", 2)
    near_a = swap(near_a, "dp", 1)
    sum_b, near_b = merge(two_b, cross_b, near_b)
    sum_b = swap(sum_b, "dp", 2)
    near_b = swap(near_b, "dp", 1)

    first_moment, second_moment, own = fixed(first_moment), fixed(second_moment), fixed(own)
    grow = functools.partial(expand, z[None], basis_cols, shape)
    rows_a, *moments = adam(own, near_a, sum_a, first_moment, second_moment, 0, None)
    far_a = swap(rows_a, "dp", 2)
    next_a = swap(rows_a, "dp", 1)
    update, token = grow(None, ((rows_a, 0, 0),))
    rows_b, *moments = adam(
        own, near_b, sum_b, first_moment, second_moment, 1, moments, (token,)
    )
    far_b = swap(rows_b, "dp", 2)
    next_b = swap(rows_b, "dp", 1)
    update, token = grow(update, ((next_a, 1, 0),))
    last_a = swap(pass_on(far_a, token), "dp", 1)
    update, token = grow(update, ((far_a, 2, 0), (rows_b, 0, 1)))
    last_b = swap(pass_on(far_b, token), "dp", 1)
    for pieces in (
        ((next_b, 1, 1), (far_b, 2, 1)),
        ((last_a, 3, 0), (last_b, 3, 1)),
    ):
        update, token = grow(update, pieces)
    return (update, *moments)


def general(activations, out_grad, basis, first_moment, second_moment):
    features = out_grad.shape[1]
    fsdp_index = lax.axis_index("fsdp")
    basis_rows = lax.dynamic_slice_in_dim(basis, fsdp_index * features, features, 0)
    partial_proj = jnp.dot(out_grad, basis_rows, preferred_element_type=jnp.float32)
    projected = lax.psum(partial_proj, "fsdp").astype(jnp.bfloat16)
    low_grad = lax.psum_scatter(
        lax.dot_general(
            activations, projected, (((0,), (0,)), ((), ())), preferred_element_type=jnp.float32
        ),
        "dp",
        scatter_dimension=0,
        tiled=True,
    )
    first_next = 0.9 * first_moment + 0.1 * low_grad
    second_next = 0.999 * second_moment + 0.001 * low_grad * low_grad
    first_fix = 1.0 - 0.9**STEP
    second_fix = 1.0 - 0.999**STEP
    normed = (first_next / first_fix / (jnp.sqrt(second_next / second_fix) + 1e-08)).astype(
        jnp.bfloat16
    )
    width = basis.shape[0] // lax.axis_size("dp")
    basis_cols = lax.dynamic_slice_in_dim(basis, lax.axis_index("dp") * width, width, 0)
    product = lax.dot_general(
        lax.all_gather(normed, "dp", axis=0, tiled=True),
        basis_cols,
        (((1,), (1,)), ((), ())),
        preferred_element_type=jnp.float32,
    )
    update = (0.25 * product).astype(jnp.bfloat16)
    return (update, first_next, second_next)


def solution(mesh):
    placed = (
        P(("groups", "dp"), "fsdp"),
        P(("groups", "dp"), "fsdp"),
        P("groups", None),
        P(("groups", "fsdp", "dp"), None),
        P(("groups", "fsdp", "dp"), None),
    )
    on_device = paired if mesh.shape["dp"] == 4 and mesh.shape["fsdp"] == 4 else general
    return jax.shard_map(
        on_device,
        mesh=mesh,
        in_specs=placed,
        out_specs=(
            P(("groups", "fsdp"), "dp"),
            P(("groups", "fsdp", "dp"), None),
            P(("groups", "fsdp", "dp"), None),
        ),
        check_vma=False,
    )
```

```python
import functools

import jax
import jax.numpy as jnp
from jax import lax
from jax.experimental import pallas as pl
from jax.experimental.pallas import tpu as pltpu
from jax.sharding import PartitionSpec as P

STEP = 10
CHUNKS = 2
VMEM = 16 << 20
WIDE = 32 << 20
PIECES = 3
TOKEN = jax.ShapeDtypeStruct((8, 128), jnp.float32)


def cost(flops, moved):
    return pl.CostEstimate(flops=flops, bytes_accessed=moved, transcendentals=0)


def swap(value, axis, bit):
    n = lax.axis_size(axis)
    return lax.ppermute(value, axis, [(i, i ^ bit) for i in range(n)])


def project_give(out_grad, basis):
    tokens, features = out_grad.shape
    rows, rank = tokens // 2, basis.shape[1]
    piece = rows // PIECES

    def kernel(grad_hbm, basis_hbm, out_ref, held, base, grad, sems):
        place = lax.axis_index("fsdp")
        core = lax.rem(place, 2)
        copies = [
            pltpu.make_async_copy(
                basis_hbm.at[pl.ds(pl.multiple_of(place * features, features), features), :],
                base,
                sems.at[0],
            )
        ]
        for turn, (half, target) in enumerate(((1 - core, grad), (core, held))):
            for part in range(PIECES):
                first = half * rows + part * piece
                copies.append(
                    pltpu.make_async_copy(
                        grad_hbm.at[pl.ds(pl.multiple_of(first, piece), piece), :],
                        target.at[pl.ds(part * piece, piece), :],
                        sems.at[turn * PIECES + part + 1],
                    )
                )
        for copy in copies:
            copy.start()
        for copy in copies[: PIECES + 1]:
            copy.wait()
        out_ref[...] = jnp.dot(
            grad[...], base[...], preferred_element_type=jnp.float32
        ).T
        for copy in copies[PIECES + 1 :]:
            copy.wait()

    return pl.pallas_call(
        kernel,
        in_specs=[pl.BlockSpec(memory_space=pltpu.HBM)] * 2,
        out_specs=[pl.BlockSpec(memory_space=pltpu.VMEM)] * 3,
        out_shape=[
            jax.ShapeDtypeStruct((rank, rows), jnp.float32),
            jax.ShapeDtypeStruct((rows, features), jnp.bfloat16),
            jax.ShapeDtypeStruct((features, rank), jnp.bfloat16),
        ],
        scratch_shapes=[
            pltpu.VMEM((rows, features), jnp.bfloat16),
            pltpu.SemaphoreType.DMA((2 * PIECES + 1,)),
        ],
        compiler_params=pltpu.CompilerParams(vmem_limit_bytes=VMEM),
        cost_estimate=cost(1000, 1000),
        name="project_give",
    )(out_grad, basis)


def project_keep(grad, base):
    rows, rank = grad.shape[0], base.shape[1]

    def kernel(grad_ref, base_ref, out_ref):
        out_ref[...] = jnp.dot(
            grad_ref[...], base_ref[...], preferred_element_type=jnp.float32
        ).T

    return pl.pallas_call(
        kernel,
        in_specs=[pl.BlockSpec(memory_space=pltpu.VMEM)] * 2,
        out_specs=pl.BlockSpec(memory_space=pltpu.VMEM),
        out_shape=jax.ShapeDtypeStruct((rank, rows), jnp.float32),
        compiler_params=pltpu.CompilerParams(vmem_limit_bytes=VMEM),
        cost_estimate=cost(1000, 1000),
        name="project_keep",
    )(grad, base)


def settle(pair, far, after):
    def kernel(pair_ref, far_ref, after_ref, out_ref):
        out_ref[...] = (pair_ref[...] + far_ref[...]).astype(jnp.bfloat16)

    return pl.pallas_call(
        kernel,
        in_specs=[pl.BlockSpec(memory_space=pltpu.VMEM)] * 2
        + [pl.BlockSpec(memory_space=pl.ANY)],
        out_specs=pl.BlockSpec(memory_space=pltpu.VMEM),
        out_shape=jax.ShapeDtypeStruct(pair.shape, jnp.bfloat16),
        compiler_params=pltpu.CompilerParams(vmem_limit_bytes=VMEM),
        cost_estimate=cost(pair.size, 10 * pair.size),
        name="settle",
    )(pair, far, after)


def merge(own, got, waiting):
    def kernel(own_ref, got_ref, waiting_ref, out_ref, next_ref):
        out_ref[...] = (own_ref[...] + got_ref[...].astype(jnp.float32)).astype(jnp.bfloat16)
        next_ref[...] = waiting_ref[...]

    return pl.pallas_call(
        kernel,
        in_specs=[pl.BlockSpec(memory_space=pltpu.VMEM)] * 3,
        out_specs=[pl.BlockSpec(memory_space=pltpu.VMEM)] * 2,
        out_shape=[
            jax.ShapeDtypeStruct(got.shape, jnp.bfloat16),
            jax.ShapeDtypeStruct(waiting.shape, jnp.bfloat16),
        ],
        compiler_params=pltpu.CompilerParams(vmem_limit_bytes=VMEM),
        cost_estimate=cost(own.size, 8 * own.size),
        name="merge",
    )(own, got, waiting)


def pass_on(value, after):
    def kernel(value_ref, after_ref, out_ref):
        out_ref[...] = value_ref[...]

    return pl.pallas_call(
        kernel,
        in_specs=[pl.BlockSpec(memory_space=pltpu.VMEM), pl.BlockSpec(memory_space=pl.ANY)],
        out_specs=pl.BlockSpec(memory_space=pltpu.VMEM),
        out_shape=jax.ShapeDtypeStruct(value.shape, value.dtype),
        compiler_params=pltpu.CompilerParams(vmem_limit_bytes=VMEM),
        cost_estimate=cost(0, 4 * value.size),
        name="pass_on",
    )(value, after)


def blocks_of(act_hbm, held, sems, parts, rows):
    copies = []
    for place, (bit, chunk) in enumerate(parts):
        block = (lax.axis_index("dp") ^ bit) * CHUNKS + chunk
        copies.append(
            pltpu.make_async_copy(
                act_hbm.at[:, pl.ds(pl.multiple_of(block * rows, 128), rows)],
                held.at[place],
                sems.at[place],
            )
        )
    for copy in copies:
        copy.start()
    return copies


def load(activations, basis, parts, after):
    tokens, units = activations.shape
    rows = units // (lax.axis_size("dp") * CHUNKS)
    width, rank = basis.shape[0] // lax.axis_size("dp"), basis.shape[1]

    def kernel(act_hbm, basis_hbm, after_ref, held, columns, token_ref, sems):
        first = pl.multiple_of(lax.axis_index("dp") * width, width)
        extra = pltpu.make_async_copy(
            basis_hbm.at[pl.ds(first, width), :], columns, sems.at[len(parts)]
        )
        extra.start()
        for copy in blocks_of(act_hbm, held, sems, parts, rows):
            copy.wait()
        extra.wait()
        token_ref[...] = jnp.zeros_like(token_ref)

    return pl.pallas_call(
        kernel,
        in_specs=[pl.BlockSpec(memory_space=pltpu.HBM)] * 2 + [pl.BlockSpec(memory_space=pl.ANY)],
        out_specs=[pl.BlockSpec(memory_space=pltpu.VMEM)] * 3,
        out_shape=[
            jax.ShapeDtypeStruct((len(parts), tokens, rows), jnp.bfloat16),
            jax.ShapeDtypeStruct((width, rank), jnp.bfloat16),
            TOKEN,
        ],
        scratch_shapes=[pltpu.SemaphoreType.DMA((len(parts) + 1,))],
        compiler_params=pltpu.CompilerParams(vmem_limit_bytes=VMEM),
        cost_estimate=cost(0, 2 * tokens * rows * len(parts)),
        name="load",
    )(activations, basis, after)


def term(mine_ref, other_ref, block):
    first = lax.rem(lax.axis_index("fsdp"), 2) == 0
    low, high = mine_ref[...], other_ref[...]
    whole = jnp.concatenate(
        [jnp.where(first, low, high), jnp.where(first, high, low)], axis=1
    )
    return jnp.dot(whole, block, preferred_element_type=jnp.float32).T


def low_held(held, mine, other, place, after):
    rank = mine.shape[0]
    _, tokens, rows = held.shape

    def kernel(mine_ref, other_ref, act_ref, after_ref, out_ref, token_ref):
        out_ref[...] = term(mine_ref, other_ref, act_ref[place]).astype(jnp.bfloat16)
        token_ref[...] = jnp.zeros_like(token_ref)

    return pl.pallas_call(
        kernel,
        in_specs=[pl.BlockSpec(memory_space=pltpu.VMEM)] * 3
        + [pl.BlockSpec(memory_space=pl.ANY)],
        out_specs=[pl.BlockSpec(memory_space=pltpu.VMEM)] * 2,
        out_shape=[jax.ShapeDtypeStruct((rows, rank), jnp.bfloat16), TOKEN],
        compiler_params=pltpu.CompilerParams(vmem_limit_bytes=VMEM),
        cost_estimate=cost(2 * tokens * rows * rank, 2 * tokens * rows),
        name="low_held",
    )(mine, other, held, after)


def low_rest(activations, mine, other, groups, after):
    rank = mine.shape[0]
    tokens, units = activations.shape
    rows = units // (lax.axis_size("dp") * CHUNKS)
    parts = [part for _, _, blocks in groups for part in blocks]

    def kernel(mine_ref, other_ref, act_hbm, after_ref, *rest):
        held, sems = rest[-2:]
        copies = blocks_of(act_hbm, held, sems, parts, rows)
        place = 0
        for out_ref, (kind, _, blocks) in zip(rest, groups):
            for row in range(len(blocks)):
                copies[place].wait()
                out_ref[row * rows : (row + 1) * rows, :] = term(
                    mine_ref, other_ref, held[place]
                ).astype(kind)
                place += 1

    shapes = [(len(blocks) * rows, rank) for _, _, blocks in groups]
    return pl.pallas_call(
        kernel,
        grid=(1,),
        in_specs=[pl.BlockSpec(memory_space=pltpu.VMEM)] * 2
        + [pl.BlockSpec(memory_space=pltpu.HBM), pl.BlockSpec(memory_space=pl.ANY)],
        out_specs=[pl.BlockSpec(shape, lambda i: (0, 0)) for shape in shapes],
        out_shape=[memory(shape, kind) for shape, (kind, memory, _) in zip(shapes, groups)],
        scratch_shapes=[
            pltpu.VMEM((len(parts), tokens, rows), jnp.bfloat16),
            pltpu.SemaphoreType.DMA((len(parts),)),
        ],
        compiler_params=pltpu.CompilerParams(vmem_limit_bytes=WIDE),
        cost_estimate=cost(1000, 1000),
        name="low_rest",
    )(mine, other, activations, after)


def bring(arrays, after):
    count = len(arrays)

    def kernel(*refs):
        sems = refs[-1]
        copies = [
            pltpu.make_async_copy(refs[place], refs[count + 1 + place], sems.at[place])
            for place in range(count)
        ]
        for copy in copies:
            copy.start()
        for copy in copies:
            copy.wait()

    return pl.pallas_call(
        kernel,
        in_specs=[pl.BlockSpec(memory_space=pltpu.HBM)] * count
        + [pl.BlockSpec(memory_space=pl.ANY)],
        out_specs=[pl.BlockSpec(memory_space=pltpu.VMEM)] * count,
        out_shape=[jax.ShapeDtypeStruct(array.shape, array.dtype) for array in arrays],
        scratch_shapes=[pltpu.SemaphoreType.DMA((count,))],
        compiler_params=pltpu.CompilerParams(vmem_limit_bytes=VMEM),
        cost_estimate=cost(0, 1000),
        name="bring",
    )(*arrays, after)


def adam(own, near, far, first, second, chunk, before, after=()):
    rows, rank = far.shape
    tile = rows // 2
    first_fix = 1.0 - 0.9**STEP
    second_fix = 1.0 - 0.999**STEP

    def kernel(own_ref, near_ref, far_ref, first_ref, second_ref, *rest):
        normed_ref, first_out, second_out = rest[-3:]
        low = (
            own_ref[...]
            + near_ref[...].astype(jnp.float32)
            + far_ref[...].astype(jnp.float32)
        )
        first_next = 0.9 * first_ref[...] + 0.1 * low
        second_next = 0.999 * second_ref[...] + 0.001 * low * low
        first_out[...] = first_next
        second_out[...] = second_next
        normed_ref[...] = (
            first_next / first_fix / (jnp.sqrt(second_next / second_fix) + 1e-08)
        ).astype(jnp.bfloat16)

    local = pl.BlockSpec((tile, rank), lambda i: (i, 0))
    whole = pl.BlockSpec((tile, rank), lambda i: (chunk * 2 + i, 0))
    extra = [] if before is None else list(before)
    return pl.pallas_call(
        kernel,
        grid=(2,),
        in_specs=[whole, local, local, whole, whole]
        + [pl.BlockSpec(memory_space=pl.ANY)] * (len(extra) + len(after)),
        out_specs=[local, whole, whole],
        out_shape=[
            jax.ShapeDtypeStruct((rows, rank), jnp.bfloat16),
            jax.ShapeDtypeStruct(first.shape, jnp.float32),
            jax.ShapeDtypeStruct(second.shape, jnp.float32),
        ],
        input_output_aliases={5: 1, 6: 2} if extra else {},
        compiler_params=pltpu.CompilerParams(vmem_limit_bytes=VMEM),
        cost_estimate=cost(30 * rows * rank, 24 * rows * rank),
        name="adam",
    )(own, near, far, first, second, *extra, *after)


def expand(place, basis_cols, shape, before, pieces):
    rows, rank = pieces[0][0].shape
    width = basis_cols.shape[0]
    steps = 2
    tile = rows // steps
    count = len(pieces)

    def block(i, s):
        place = jnp.int32(0)
        for turn, (_, bit, chunk) in enumerate(pieces):
            here = ((s[0] ^ bit) * CHUNKS + chunk) * steps + i - turn * steps
            place = here if turn == 0 else jnp.where(i >= turn * steps, here, place)
        return place, 0

    def kernel(s, basis_ref, *rest):
        out_ref, token_ref = rest[-2:]
        step = pl.program_id(0)
        for turn in range(count):

            @pl.when(step // steps == turn)
            def _():
                product = lax.dot_general(
                    rest[turn][...],
                    basis_ref[...],
                    (((1,), (1,)), ((), ())),
                    preferred_element_type=jnp.float32,
                )
                out_ref[...] = (0.25 * product).astype(jnp.bfloat16)

        token_ref[...] = jnp.zeros_like(token_ref)

    def rows_of(turn):
        return lambda i, s: (jnp.clip(i - turn * steps, 0, steps - 1), 0)

    extra = [] if before is None else [before]
    return pl.pallas_call(
        kernel,
        grid_spec=pltpu.PrefetchScalarGridSpec(
            num_scalar_prefetch=1,
            grid=(count * steps,),
            in_specs=[pl.BlockSpec((width, rank), lambda i, s: (0, 0))]
            + [pl.BlockSpec((tile, rank), rows_of(turn)) for turn in range(count)]
            + [pl.BlockSpec(memory_space=pl.ANY)] * len(extra),
            out_specs=[
                pl.BlockSpec((tile, width), block),
                pl.BlockSpec((8, 128), lambda i, s: (0, 0)),
            ],
        ),
        out_shape=[jax.ShapeDtypeStruct(shape, jnp.bfloat16), TOKEN],
        input_output_aliases={2 + count: 0} if extra else {},
        compiler_params=pltpu.CompilerParams(vmem_limit_bytes=VMEM),
        cost_estimate=cost(60 * rows * rank * width * count, 60 * rows * width * count),
        name="expand",
    )(place, basis_cols, *[piece for piece, _, _ in pieces], *extra)


def paired(activations, out_grad, basis, first_moment, second_moment):
    f32, b16 = jnp.float32, jnp.bfloat16
    z = lax.axis_index("dp")
    width = basis.shape[0] // lax.axis_size("dp")
    fixed = functools.partial(pltpu.with_memory_space_constraint, memory_space=pltpu.HBM)
    shape = (activations.shape[1], width)
    out_grad, activations, basis = fixed(out_grad), fixed(activations), fixed(basis)
    give, grad, base = project_give(out_grad, basis)
    keep = project_keep(grad, base)
    held, basis_cols, token = load(activations, basis, ((3, 0), (3, 1)), keep)
    pair = keep + swap(give, "fsdp", 1)
    mine = settle(pair, swap(pair, "fsdp", 2), token)
    other = swap(mine, "fsdp", 1)

    cross_a, token = low_held(held, mine, other, 0, token)
    cross_a = swap(cross_a, "dp", 1)
    cross_b, token = low_held(held, mine, other, 1, token)
    cross_b = swap(cross_b, "dp", 1)
    plain = jax.ShapeDtypeStruct
    two_a, near_a, two_b, near_b, own = low_rest(
        activations,
        mine,
        other,
        (
            (f32, plain, ((2, 0),)),
            (b16, plain, ((1, 0),)),
            (f32, plain, ((2, 1),)),
            (b16, plain, ((1, 1),)),
            (f32, pltpu.HBM, ((0, 0), (0, 1))),
        ),
        token,
    )
    sum_a, near_a = merge(two_a, cross_a, near_a)
    first_moment, second_moment, own = bring(
        (fixed(first_moment), fixed(second_moment), fixed(own)), sum_a
    )
    sum_a = swap(sum_a, "dp", 2)
    near_a = swap(near_a, "dp", 1)
    sum_b, near_b = merge(two_b, cross_b, near_b)
    sum_b = swap(sum_b, "dp", 2)
    near_b = swap(near_b, "dp", 1)

    grow = functools.partial(expand, z[None], basis_cols, shape)
    rows_a, *moments = adam(own, near_a, sum_a, first_moment, second_moment, 0, None)
    far_a = swap(rows_a, "dp", 2)
    next_a = swap(rows_a, "dp", 1)
    update, token = grow(None, ((rows_a, 0, 0),))
    rows_b, *moments = adam(
        own, near_b, sum_b, first_moment, second_moment, 1, moments, (token,)
    )
    far_b = swap(rows_b, "dp", 2)
    next_b = swap(rows_b, "dp", 1)
    update, token = grow(update, ((next_a, 1, 0),))
    last_a = swap(pass_on(far_a, token), "dp", 1)
    update, token = grow(update, ((far_a, 2, 0), (rows_b, 0, 1)))
    last_b = swap(pass_on(far_b, token), "dp", 1)
    for pieces in (
        ((next_b, 1, 1), (far_b, 2, 1)),
        ((last_a, 3, 0), (last_b, 3, 1)),
    ):
        update, token = grow(update, pieces)
    return (update, *moments)


def general(activations, out_grad, basis, first_moment, second_moment):
    features = out_grad.shape[1]
    fsdp_index = lax.axis_index("fsdp")
    basis_rows = lax.dynamic_slice_in_dim(basis, fsdp_index * features, features, 0)
    partial_proj = jnp.dot(out_grad, basis_rows, preferred_element_type=jnp.float32)
    projected = lax.psum(partial_proj, "fsdp").astype(jnp.bfloat16)
    low_grad = lax.psum_scatter(
        lax.dot_general(
            activations, projected, (((0,), (0,)), ((), ())), preferred_element_type=jnp.float32
        ),
        "dp",
        scatter_dimension=0,
        tiled=True,
    )
    first_next = 0.9 * first_moment + 0.1 * low_grad
    second_next = 0.999 * second_moment + 0.001 * low_grad * low_grad
    first_fix = 1.0 - 0.9**STEP
    second_fix = 1.0 - 0.999**STEP
    normed = (first_next / first_fix / (jnp.sqrt(second_next / second_fix) + 1e-08)).astype(
        jnp.bfloat16
    )
    width = basis.shape[0] // lax.axis_size("dp")
    basis_cols = lax.dynamic_slice_in_dim(basis, lax.axis_index("dp") * width, width, 0)
    product = lax.dot_general(
        lax.all_gather(normed, "dp", axis=0, tiled=True),
        basis_cols,
        (((1,), (1,)), ((), ())),
        preferred_element_type=jnp.float32,
    )
    update = (0.25 * product).astype(jnp.bfloat16)
    return (update, first_next, second_next)


def solution(mesh):
    placed = (
        P(("groups", "dp"), "fsdp"),
        P(("groups", "dp"), "fsdp"),
        P("groups", None),
        P(("groups", "fsdp", "dp"), None),
        P(("groups", "fsdp", "dp"), None),
    )
    on_device = paired if mesh.shape["dp"] == 4 and mesh.shape["fsdp"] == 4 else general
    return jax.shard_map(
        on_device,
        mesh=mesh,
        in_specs=placed,
        out_specs=(
            P(("groups", "fsdp"), "dp"),
            P(("groups", "fsdp", "dp"), None),
            P(("groups", "fsdp", "dp"), None),
        ),
        check_vma=False,
    )
```

```python
import functools

import jax
import jax.numpy as jnp
from jax import lax
from jax.experimental import pallas as pl
from jax.experimental.pallas import tpu as pltpu
from jax.sharding import PartitionSpec as P

STEP = 10
CHUNKS = 2
VMEM = 16 << 20
WIDE = 32 << 20
PIECES = 3
TOKEN = jax.ShapeDtypeStruct((8, 128), jnp.float32)


def cost(flops, moved):
    return pl.CostEstimate(flops=flops, bytes_accessed=moved, transcendentals=0)


def swap(value, axis, bit):
    n = lax.axis_size(axis)
    return lax.ppermute(value, axis, [(i, i ^ bit) for i in range(n)])


def project_give(out_grad, basis):
    tokens, features = out_grad.shape
    rows, rank = tokens // 2, basis.shape[1]
    piece = rows // PIECES

    def kernel(grad_hbm, basis_hbm, out_ref, held, base, grad, sems):
        place = lax.axis_index("fsdp")
        core = lax.rem(place, 2)
        copies = [
            pltpu.make_async_copy(
                basis_hbm.at[pl.ds(pl.multiple_of(place * features, features), features), :],
                base,
                sems.at[0],
            )
        ]
        for turn, (half, target) in enumerate(((1 - core, grad), (core, held))):
            for part in range(PIECES):
                first = half * rows + part * piece
                copies.append(
                    pltpu.make_async_copy(
                        grad_hbm.at[pl.ds(pl.multiple_of(first, piece), piece), :],
                        target.at[pl.ds(part * piece, piece), :],
                        sems.at[turn * PIECES + part + 1],
                    )
                )
        for copy in copies:
            copy.start()
        for copy in copies[: PIECES + 1]:
            copy.wait()
        out_ref[...] = jnp.dot(
            grad[...], base[...], preferred_element_type=jnp.float32
        ).T
        for copy in copies[PIECES + 1 :]:
            copy.wait()

    return pl.pallas_call(
        kernel,
        in_specs=[pl.BlockSpec(memory_space=pltpu.HBM)] * 2,
        out_specs=[pl.BlockSpec(memory_space=pltpu.VMEM)] * 3,
        out_shape=[
            jax.ShapeDtypeStruct((rank, rows), jnp.float32),
            jax.ShapeDtypeStruct((rows, features), jnp.bfloat16),
            jax.ShapeDtypeStruct((features, rank), jnp.bfloat16),
        ],
        scratch_shapes=[
            pltpu.VMEM((rows, features), jnp.bfloat16),
            pltpu.SemaphoreType.DMA((2 * PIECES + 1,)),
        ],
        compiler_params=pltpu.CompilerParams(vmem_limit_bytes=VMEM),
        cost_estimate=cost(1000, 1000),
        name="project_give",
    )(out_grad, basis)


def project_keep(grad, base):
    rows, rank = grad.shape[0], base.shape[1]

    def kernel(grad_ref, base_ref, out_ref):
        out_ref[...] = jnp.dot(
            grad_ref[...], base_ref[...], preferred_element_type=jnp.float32
        ).T

    return pl.pallas_call(
        kernel,
        in_specs=[pl.BlockSpec(memory_space=pltpu.VMEM)] * 2,
        out_specs=pl.BlockSpec(memory_space=pltpu.VMEM),
        out_shape=jax.ShapeDtypeStruct((rank, rows), jnp.float32),
        compiler_params=pltpu.CompilerParams(vmem_limit_bytes=VMEM),
        cost_estimate=cost(1000, 1000),
        name="project_keep",
    )(grad, base)


def settle(pair, far, after):
    def kernel(pair_ref, far_ref, after_ref, out_ref):
        out_ref[...] = (pair_ref[...] + far_ref[...]).astype(jnp.bfloat16)

    return pl.pallas_call(
        kernel,
        in_specs=[pl.BlockSpec(memory_space=pltpu.VMEM)] * 2
        + [pl.BlockSpec(memory_space=pl.ANY)],
        out_specs=pl.BlockSpec(memory_space=pltpu.VMEM),
        out_shape=jax.ShapeDtypeStruct(pair.shape, jnp.bfloat16),
        compiler_params=pltpu.CompilerParams(vmem_limit_bytes=VMEM),
        cost_estimate=cost(pair.size, 10 * pair.size),
        name="settle",
    )(pair, far, after)


def merge(own, got, waiting):
    def kernel(own_ref, got_ref, waiting_ref, out_ref, next_ref):
        out_ref[...] = (own_ref[...] + got_ref[...].astype(jnp.float32)).astype(jnp.bfloat16)
        next_ref[...] = waiting_ref[...]

    return pl.pallas_call(
        kernel,
        in_specs=[pl.BlockSpec(memory_space=pltpu.VMEM)] * 3,
        out_specs=[pl.BlockSpec(memory_space=pltpu.VMEM)] * 2,
        out_shape=[
            jax.ShapeDtypeStruct(got.shape, jnp.bfloat16),
            jax.ShapeDtypeStruct(waiting.shape, jnp.bfloat16),
        ],
        compiler_params=pltpu.CompilerParams(vmem_limit_bytes=VMEM),
        cost_estimate=cost(own.size, 8 * own.size),
        name="merge",
    )(own, got, waiting)


def pass_on(value, after):
    def kernel(value_ref, after_ref, out_ref):
        out_ref[...] = value_ref[...]

    return pl.pallas_call(
        kernel,
        in_specs=[pl.BlockSpec(memory_space=pltpu.VMEM), pl.BlockSpec(memory_space=pl.ANY)],
        out_specs=pl.BlockSpec(memory_space=pltpu.VMEM),
        out_shape=jax.ShapeDtypeStruct(value.shape, value.dtype),
        compiler_params=pltpu.CompilerParams(vmem_limit_bytes=VMEM),
        cost_estimate=cost(0, 4 * value.size),
        name="pass_on",
    )(value, after)


def blocks_of(act_hbm, held, sems, parts, rows):
    copies = []
    for place, (bit, chunk) in enumerate(parts):
        block = (lax.axis_index("dp") ^ bit) * CHUNKS + chunk
        copies.append(
            pltpu.make_async_copy(
                act_hbm.at[:, pl.ds(pl.multiple_of(block * rows, 128), rows)],
                held.at[place],
                sems.at[place],
            )
        )
    for copy in copies:
        copy.start()
    return copies


def load(activations, basis, parts, after):
    tokens, units = activations.shape
    rows = units // (lax.axis_size("dp") * CHUNKS)
    width, rank = basis.shape[0] // lax.axis_size("dp"), basis.shape[1]

    def kernel(act_hbm, basis_hbm, after_ref, held, columns, token_ref, sems):
        first = pl.multiple_of(lax.axis_index("dp") * width, width)
        extra = pltpu.make_async_copy(
            basis_hbm.at[pl.ds(first, width), :], columns, sems.at[len(parts)]
        )
        extra.start()
        for copy in blocks_of(act_hbm, held, sems, parts, rows):
            copy.wait()
        extra.wait()
        token_ref[...] = jnp.zeros_like(token_ref)

    return pl.pallas_call(
        kernel,
        in_specs=[pl.BlockSpec(memory_space=pltpu.HBM)] * 2 + [pl.BlockSpec(memory_space=pl.ANY)],
        out_specs=[pl.BlockSpec(memory_space=pltpu.VMEM)] * 3,
        out_shape=[
            jax.ShapeDtypeStruct((len(parts), tokens, rows), jnp.bfloat16),
            jax.ShapeDtypeStruct((width, rank), jnp.bfloat16),
            TOKEN,
        ],
        scratch_shapes=[pltpu.SemaphoreType.DMA((len(parts) + 1,))],
        compiler_params=pltpu.CompilerParams(vmem_limit_bytes=VMEM),
        cost_estimate=cost(0, 2 * tokens * rows * len(parts)),
        name="load",
    )(activations, basis, after)


def term(mine_ref, other_ref, block):
    first = lax.rem(lax.axis_index("fsdp"), 2) == 0
    low, high = mine_ref[...], other_ref[...]
    whole = jnp.concatenate(
        [jnp.where(first, low, high), jnp.where(first, high, low)], axis=1
    )
    return jnp.dot(whole, block, preferred_element_type=jnp.float32).T


def low_held(held, mine, other, place, after):
    rank = mine.shape[0]
    _, tokens, rows = held.shape

    def kernel(mine_ref, other_ref, act_ref, after_ref, out_ref, token_ref):
        out_ref[...] = term(mine_ref, other_ref, act_ref[place]).astype(jnp.bfloat16)
        token_ref[...] = jnp.zeros_like(token_ref)

    return pl.pallas_call(
        kernel,
        in_specs=[pl.BlockSpec(memory_space=pltpu.VMEM)] * 3
        + [pl.BlockSpec(memory_space=pl.ANY)],
        out_specs=[pl.BlockSpec(memory_space=pltpu.VMEM)] * 2,
        out_shape=[jax.ShapeDtypeStruct((rows, rank), jnp.bfloat16), TOKEN],
        compiler_params=pltpu.CompilerParams(vmem_limit_bytes=VMEM),
        cost_estimate=cost(2 * tokens * rows * rank, 2 * tokens * rows),
        name="low_held",
    )(mine, other, held, after)


def low_rest(activations, mine, other, groups, after):
    rank = mine.shape[0]
    tokens, units = activations.shape
    rows = units // (lax.axis_size("dp") * CHUNKS)
    parts = [part for _, _, blocks in groups for part in blocks]

    def kernel(mine_ref, other_ref, act_hbm, after_ref, *rest):
        held, sems = rest[-2:]
        copies = blocks_of(act_hbm, held, sems, parts, rows)
        place = 0
        for out_ref, (kind, _, blocks) in zip(rest, groups):
            for row in range(len(blocks)):
                copies[place].wait()
                out_ref[row * rows : (row + 1) * rows, :] = term(
                    mine_ref, other_ref, held[place]
                ).astype(kind)
                place += 1

    shapes = [(len(blocks) * rows, rank) for _, _, blocks in groups]
    return pl.pallas_call(
        kernel,
        grid=(1,),
        in_specs=[pl.BlockSpec(memory_space=pltpu.VMEM)] * 2
        + [pl.BlockSpec(memory_space=pltpu.HBM), pl.BlockSpec(memory_space=pl.ANY)],
        out_specs=[pl.BlockSpec(shape, lambda i: (0, 0)) for shape in shapes],
        out_shape=[memory(shape, kind) for shape, (kind, memory, _) in zip(shapes, groups)],
        scratch_shapes=[
            pltpu.VMEM((len(parts), tokens, rows), jnp.bfloat16),
            pltpu.SemaphoreType.DMA((len(parts),)),
        ],
        compiler_params=pltpu.CompilerParams(vmem_limit_bytes=WIDE),
        cost_estimate=cost(1000, 1000),
        name="low_rest",
    )(mine, other, activations, after)


def bring(arrays, after):
    count = len(arrays)

    def kernel(*refs):
        sems = refs[-1]
        copies = [
            pltpu.make_async_copy(refs[place], refs[count + 1 + place], sems.at[place])
            for place in range(count)
        ]
        for copy in copies:
            copy.start()
        for copy in copies:
            copy.wait()

    return pl.pallas_call(
        kernel,
        in_specs=[pl.BlockSpec(memory_space=pltpu.HBM)] * count
        + [pl.BlockSpec(memory_space=pl.ANY)],
        out_specs=[pl.BlockSpec(memory_space=pltpu.VMEM)] * count,
        out_shape=[jax.ShapeDtypeStruct(array.shape, array.dtype) for array in arrays],
        scratch_shapes=[pltpu.SemaphoreType.DMA((count,))],
        compiler_params=pltpu.CompilerParams(vmem_limit_bytes=VMEM),
        cost_estimate=cost(0, 1000),
        name="bring",
    )(*arrays, after)


def adam(own, near, far, first, second, chunk, before, after=()):
    rows, rank = far.shape
    tile = rows
    first_fix = 1.0 - 0.9**STEP
    second_fix = 1.0 - 0.999**STEP

    def kernel(own_ref, near_ref, far_ref, first_ref, second_ref, *rest):
        normed_ref, first_out, second_out = rest[-3:]
        low = (
            own_ref[...]
            + near_ref[...].astype(jnp.float32)
            + far_ref[...].astype(jnp.float32)
        )
        first_next = 0.9 * first_ref[...] + 0.1 * low
        second_next = 0.999 * second_ref[...] + 0.001 * low * low
        first_out[...] = first_next
        second_out[...] = second_next
        normed_ref[...] = (
            first_next / first_fix / (jnp.sqrt(second_next / second_fix) + 1e-08)
        ).astype(jnp.bfloat16)

    local = pl.BlockSpec((tile, rank), lambda i: (i, 0))
    whole = pl.BlockSpec((tile, rank), lambda i: (chunk + i, 0))
    extra = [] if before is None else list(before)
    return pl.pallas_call(
        kernel,
        grid=(1,),
        in_specs=[whole, local, local, whole, whole]
        + [pl.BlockSpec(memory_space=pl.ANY)] * (len(extra) + len(after)),
        out_specs=[local, whole, whole],
        out_shape=[
            jax.ShapeDtypeStruct((rows, rank), jnp.bfloat16),
            jax.ShapeDtypeStruct(first.shape, jnp.float32),
            jax.ShapeDtypeStruct(second.shape, jnp.float32),
        ],
        input_output_aliases={5: 1, 6: 2} if extra else {},
        compiler_params=pltpu.CompilerParams(vmem_limit_bytes=VMEM),
        cost_estimate=cost(30 * rows * rank, 24 * rows * rank),
        name="adam",
    )(own, near, far, first, second, *extra, *after)


def expand(place, basis_cols, shape, before, pieces):
    rows, rank = pieces[0][0].shape
    width = basis_cols.shape[0]
    steps = 2
    tile = rows // steps
    count = len(pieces)

    def block(i, s):
        place = jnp.int32(0)
        for turn, (_, bit, chunk) in enumerate(pieces):
            here = ((s[0] ^ bit) * CHUNKS + chunk) * steps + i - turn * steps
            place = here if turn == 0 else jnp.where(i >= turn * steps, here, place)
        return place, 0

    def kernel(s, basis_ref, *rest):
        out_ref, token_ref = rest[-2:]
        step = pl.program_id(0)
        for turn in range(count):

            @pl.when(step // steps == turn)
            def _():
                product = lax.dot_general(
                    rest[turn][...],
                    basis_ref[...],
                    (((1,), (1,)), ((), ())),
                    preferred_element_type=jnp.float32,
                )
                out_ref[...] = (0.25 * product).astype(jnp.bfloat16)

        token_ref[...] = jnp.zeros_like(token_ref)

    def rows_of(turn):
        return lambda i, s: (jnp.clip(i - turn * steps, 0, steps - 1), 0)

    extra = [] if before is None else [before]
    return pl.pallas_call(
        kernel,
        grid_spec=pltpu.PrefetchScalarGridSpec(
            num_scalar_prefetch=1,
            grid=(count * steps,),
            in_specs=[pl.BlockSpec((width, rank), lambda i, s: (0, 0))]
            + [pl.BlockSpec((tile, rank), rows_of(turn)) for turn in range(count)]
            + [pl.BlockSpec(memory_space=pl.ANY)] * len(extra),
            out_specs=[
                pl.BlockSpec((tile, width), block),
                pl.BlockSpec((8, 128), lambda i, s: (0, 0)),
            ],
        ),
        out_shape=[jax.ShapeDtypeStruct(shape, jnp.bfloat16), TOKEN],
        input_output_aliases={2 + count: 0} if extra else {},
        compiler_params=pltpu.CompilerParams(vmem_limit_bytes=VMEM),
        cost_estimate=cost(60 * rows * rank * width * count, 60 * rows * width * count),
        name="expand",
    )(place, basis_cols, *[piece for piece, _, _ in pieces], *extra)


def paired(activations, out_grad, basis, first_moment, second_moment):
    f32, b16 = jnp.float32, jnp.bfloat16
    z = lax.axis_index("dp")
    width = basis.shape[0] // lax.axis_size("dp")
    fixed = functools.partial(pltpu.with_memory_space_constraint, memory_space=pltpu.HBM)
    shape = (activations.shape[1], width)
    out_grad, activations, basis = fixed(out_grad), fixed(activations), fixed(basis)
    give, grad, base = project_give(out_grad, basis)
    keep = project_keep(grad, base)
    held, basis_cols, token = load(activations, basis, ((3, 0), (3, 1)), keep)
    pair = keep + swap(give, "fsdp", 1)
    mine = settle(pair, swap(pair, "fsdp", 2), token)
    other = swap(mine, "fsdp", 1)

    cross_a, token = low_held(held, mine, other, 0, token)
    cross_a = swap(cross_a, "dp", 1)
    cross_b, token = low_held(held, mine, other, 1, token)
    cross_b = swap(cross_b, "dp", 1)
    plain = jax.ShapeDtypeStruct
    two_a, near_a, two_b, near_b, own = low_rest(
        activations,
        mine,
        other,
        (
            (f32, plain, ((2, 0),)),
            (b16, plain, ((1, 0),)),
            (f32, plain, ((2, 1),)),
            (b16, plain, ((1, 1),)),
            (f32, pltpu.HBM, ((0, 0), (0, 1))),
        ),
        token,
    )
    sum_a, near_a = merge(two_a, cross_a, near_a)
    first_moment, second_moment, own = bring(
        (fixed(first_moment), fixed(second_moment), fixed(own)), sum_a
    )
    sum_a = swap(sum_a, "dp", 2)
    near_a = swap(near_a, "dp", 1)
    sum_b, near_b = merge(two_b, cross_b, near_b)
    sum_b = swap(sum_b, "dp", 2)
    near_b = swap(near_b, "dp", 1)

    grow = functools.partial(expand, z[None], basis_cols, shape)
    rows_a, *moments = adam(own, near_a, sum_a, first_moment, second_moment, 0, None)
    far_a = swap(rows_a, "dp", 2)
    next_a = swap(rows_a, "dp", 1)
    update, token = grow(None, ((rows_a, 0, 0),))
    rows_b, *moments = adam(
        own, near_b, sum_b, first_moment, second_moment, 1, moments, (token,)
    )
    far_b = swap(rows_b, "dp", 2)
    next_b = swap(rows_b, "dp", 1)
    update, token = grow(update, ((next_a, 1, 0),))
    last_a = swap(pass_on(far_a, token), "dp", 1)
    update, token = grow(update, ((far_a, 2, 0), (rows_b, 0, 1)))
    last_b = swap(pass_on(far_b, token), "dp", 1)
    for pieces in (
        ((next_b, 1, 1), (far_b, 2, 1)),
        ((last_a, 3, 0), (last_b, 3, 1)),
    ):
        update, token = grow(update, pieces)
    return (update, *moments)


def general(activations, out_grad, basis, first_moment, second_moment):
    features = out_grad.shape[1]
    fsdp_index = lax.axis_index("fsdp")
    basis_rows = lax.dynamic_slice_in_dim(basis, fsdp_index * features, features, 0)
    partial_proj = jnp.dot(out_grad, basis_rows, preferred_element_type=jnp.float32)
    projected = lax.psum(partial_proj, "fsdp").astype(jnp.bfloat16)
    low_grad = lax.psum_scatter(
        lax.dot_general(
            activations, projected, (((0,), (0,)), ((), ())), preferred_element_type=jnp.float32
        ),
        "dp",
        scatter_dimension=0,
        tiled=True,
    )
    first_next = 0.9 * first_moment + 0.1 * low_grad
    second_next = 0.999 * second_moment + 0.001 * low_grad * low_grad
    first_fix = 1.0 - 0.9**STEP
    second_fix = 1.0 - 0.999**STEP
    normed = (first_next / first_fix / (jnp.sqrt(second_next / second_fix) + 1e-08)).astype(
        jnp.bfloat16
    )
    width = basis.shape[0] // lax.axis_size("dp")
    basis_cols = lax.dynamic_slice_in_dim(basis, lax.axis_index("dp") * width, width, 0)
    product = lax.dot_general(
        lax.all_gather(normed, "dp", axis=0, tiled=True),
        basis_cols,
        (((1,), (1,)), ((), ())),
        preferred_element_type=jnp.float32,
    )
    update = (0.25 * product).astype(jnp.bfloat16)
    return (update, first_next, second_next)


def solution(mesh):
    placed = (
        P(("groups", "dp"), "fsdp"),
        P(("groups", "dp"), "fsdp"),
        P("groups", None),
        P(("groups", "fsdp", "dp"), None),
        P(("groups", "fsdp", "dp"), None),
    )
    on_device = paired if mesh.shape["dp"] == 4 and mesh.shape["fsdp"] == 4 else general
    return jax.shard_map(
        on_device,
        mesh=mesh,
        in_specs=placed,
        out_specs=(
            P(("groups", "fsdp"), "dp"),
            P(("groups", "fsdp", "dp"), None),
            P(("groups", "fsdp", "dp"), None),
        ),
        check_vma=False,
    )
```
